32 devices in a mesh: section: 2 (over core), dp: 16 (over z, y, x).
Axes of the slice: x: 2, y: 2, z: 4, core: 2. Of those that a mesh axis runs over, the one named last changes fastest.
Arguments:
- ends_in: bfloat16 [2, 32, 197, 384], P('section', 'dp'), may hold values from -6 to 6
- vectors: bfloat16 [2, 8, 384], P('section', None, 'dp'), may hold values from -1 to 1
- up_bias: bfloat16 [2, 1536], P('section', 'dp'), may hold values from -2 to 2
- w_qkv: bfloat16 [2, 384, 1152], P('section', 'dp'), may hold values from -0.3125 to 0.3125
- w_out: bfloat16 [2, 384, 384], P('section', 'dp'), may hold values from -0.875 to 0.875
- w_up: bfloat16 [2, 384, 1536], P('section', 'dp'), may hold values from -0.3125 to 0.3125
- w_down: bfloat16 [2, 1536, 384], P('section', 'dp'), may hold values from -0.15625 to 0.15625
Outputs:
- ends: bfloat16 [2, 32, 197, 384], P('section', 'dp')
- vectors_grad: float32 [2, 8, 384], P('section', None, 'dp')
- up_bias_grad: float32 [2, 1536], P('section', 'dp')
- w_qkv_grad: float32 [2, 384, 1152], P('section', 'dp')
- w_out_grad: float32 [2, 384, 384], P('section', 'dp')
- w_up_grad: float32 [2, 384, 1536], P('section', 'dp')
- w_down_grad: float32 [2, 1536, 384], P('section', 'dp')
The draws below stay inside these ranges and needn't reach their ends.
All inputs are finite; a program needn't handle non-finite values.
Results may differ from the reference program's by a relative error of at most 0.012.
Values may be sent and summed in bfloat16 or wider, within the bound.
A program may use at most 128 MiB of HBM per device.

```python
import jax
import jax.numpy as jnp
from jax import lax

D = 384
HEADS = 6
HEAD_DIM = 64
FF = 1536
SEQ = 197
VEC_ROWS = 8
IMG_DEV = 2
IMAGES = 32
N_SECTION = 2
N_DP = 16


def levels(rng, dims, shards, least, top_value):
    loudness, own = 1.0, jax.random.fold_in(rng, 6)
    for axis_at, shards_of in shards:
        draws = jnp.exp(jax.random.uniform(jax.random.fold_in(own, axis_at), (shards_of,), jnp.float32, least / len(shards), top_value / len(shards)))
        loudness = loudness * jnp.repeat(draws, dims[axis_at] // shards_of).reshape([-1 if axis == axis_at else 1 for axis in range(len(dims))])
    return loudness


def centred(own_key, dims, width, reach, shards=(), held_as=jnp.bfloat16):
    values = width * jax.random.normal(own_key, dims, jnp.float32)
    if shards:
        values = values * levels(own_key, dims, shards, -0.22, 0.18)
    return jnp.clip(values, -reach, reach).astype(held_as)


def setup_inputs(seed: int = 0) -> dict:
    splits = jax.random.split(jax.random.key(seed), 8)
    ends_in = centred(splits[0], (N_SECTION, IMAGES, SEQ, D), 1.0, 6.0, ((0, 2), (1, 16)))
    vectors = centred(splits[1], (N_SECTION, VEC_ROWS, D), 0.25, 1.0, ((0, 2), (2, 16)))
    up_bias = centred(splits[2], (N_SECTION, FF), 0.5, 2.0, ((0, 2), (1, 16)))
    w_qkv = centred(splits[3], (N_SECTION, D, 3 * D), D ** -0.5, 0.3125, ((0, 2), (1, 16)))
    w_out = centred(splits[4], (N_SECTION, D, D), (D // 8) ** -0.5, 0.875, ((0, 2), (1, 16)))
    w_up = centred(splits[5], (N_SECTION, D, FF), D ** -0.5, 0.3125, ((0, 2), (1, 16)))
    w_down = centred(splits[6], (N_SECTION, FF, D), FF ** -0.5, 0.15625, ((0, 2), (1, 16)))
    return dict(ends_in=ends_in, vectors=vectors, up_bias=up_bias, w_qkv=w_qkv, w_out=w_out, w_up=w_up, w_down=w_down)


@jax.custom_vjp
def low(v):
    return lax.optimization_barrier(v.astype(jnp.bfloat16)).astype(jnp.float32)

@jax.custom_vjp
def low_back(v):
    return v

def low_keep(v):
    return (low(v), None)

def low_pass(kept, grad):
    return (grad,)

def back_keep(v):
    return (v, None)

def back_low(kept, grad):
    return (low(grad),)
low.defvjp(low_keep, low_pass)
low_back.defvjp(back_keep, back_low)
norm_eps = 1e-06

def layer_norm(values, gain_raw, shift_vec):
    average = lax.optimization_barrier(jnp.mean(values, axis=-1, keepdims=True))
    centered = values - average
    variance = lax.optimization_barrier(jnp.mean(centered * centered, axis=-1, keepdims=True))
    return centered * lax.rsqrt(variance + norm_eps) * (1.0 + gain_raw) + shift_vec

def matmul_high(left_side, right_side):
    return jnp.dot(left_side, right_side, precision=lax.Precision.HIGHEST, preferred_element_type=jnp.float32)

def block_layer(hidden, params):
    vectors, up_bias, w_qkv, w_out, w_up, w_down = params
    row_count = hidden.shape[0]
    images = row_count // SEQ
    normed = low(layer_norm(hidden, vectors[0], vectors[1]))
    zero_bias = jnp.zeros_like(vectors[2])
    projected = low_back(low(matmul_high(normed, w_qkv) + jnp.concatenate([vectors[2], zero_bias, vectors[3]])))
    head_view = projected.reshape(images, SEQ, 3, HEADS, HEAD_DIM)
    queries = head_view[:, :, 0]
    key_heads = head_view[:, :, 1]
    value_heads = head_view[:, :, 2]
    scores = low_back(jnp.einsum('bqhd,bkhd->bhqk', queries, key_heads, precision=lax.Precision.HIGHEST) * HEAD_DIM ** (-0.5))
    weights = low(jax.nn.softmax(scores, axis=-1))
    attended = jnp.einsum('bhqk,bkhd->bqhd', weights, value_heads, precision=lax.Precision.HIGHEST)
    attended = low_back(low(attended.reshape(row_count, HEADS * HEAD_DIM)))
    branch = low_back(matmul_high(attended, w_out) + vectors[4])
    middle = hidden + branch
    normed_two = low(layer_norm(middle, vectors[5], vectors[6]))
    pre_gate = low_back(matmul_high(normed_two, w_up) + up_bias)
    activated = low(jax.nn.gelu(pre_gate, approximate=False))
    outcome = low_back(matmul_high(activated, w_down) + vectors[7])
    return middle + outcome

def two_layers(param_pair, image_group):
    between = block_layer(image_group, param_pair[0])
    between = low_back(low(between))
    return block_layer(between, param_pair[1])

def reference(ends_in, vectors, up_bias, w_qkv, w_out, w_up, w_down):
    stacked = tuple((array_item.astype(jnp.float32) for array_item in (vectors, up_bias, w_qkv, w_out, w_up, w_down)))
    param_pair = (tuple((array_item[0] for array_item in stacked)), tuple((array_item[1] for array_item in stacked)))
    images = ends_in[0].astype(jnp.float32).reshape(N_DP, IMG_DEV * SEQ, D)
    cotangent = ends_in[1].astype(jnp.float32).reshape(N_DP, IMG_DEV * SEQ, D)

    def network(inputs, pair_now):
        return lax.map(lambda image_group: jax.checkpoint(two_layers)(pair_now, image_group), inputs)
    outputs, pullback = jax.vjp(network, images, param_pair)
    grad_images, grad_pair = pullback(cotangent)
    ends = jnp.stack([grad_images.reshape(IMAGES, SEQ, D), outputs.reshape(IMAGES, SEQ, D)]).astype(jnp.bfloat16)
    grads = tuple((jnp.stack([grad_pair[0][position], grad_pair[1][position]]) for position in range(6)))
    return (ends, grads[0], grads[1], grads[2], grads[3], grads[4], grads[5])
```

```python
import functools

import jax
import jax.numpy as jnp
from jax import lax
from jax.experimental import pallas as pl
from jax.experimental.pallas import tpu as pltpu
from jax.sharding import PartitionSpec as P

HEADS = 6
HEAD_DIM = 64
PAIR = 2 * HEAD_DIM
EPS = 1e-06
SCALE = HEAD_DIM ** (-0.5)
VMEM_BYTES = 56 * 1024 * 1024

bf16 = jnp.bfloat16
f32 = jnp.float32
MESH = pl.DeviceIdType.MESH


def chip_grid(count):
    for side in range(1, count + 1):
        if 2 * side**3 == count:
            return (2 * side, side, side)
    return (count, 1, 1)


def place(dims):
    me = lax.axis_index("dp")
    _, size_y, size_x = dims
    return me // (size_y * size_x), (me // size_x) % size_y, me % size_x


def rank(dims, z, y, x):
    return (z * dims[1] + y) * dims[2] + x


def greet(dims, s, z, y, x):
    barrier = pltpu.get_barrier_semaphore()
    count = 1
    pl.semaphore_signal(barrier, inc=1, device_id={"section": 1 - s}, device_id_type=MESH)
    for axis, (size, at) in enumerate(zip(dims, (z, y, x))):
        for d in range(1, size):
            there = [z, y, x]
            there[axis] = (at + d) % size
            pl.semaphore_signal(barrier, inc=1, device_id={"dp": rank(dims, *there)}, device_id_type=MESH)
            count += 1
    pl.semaphore_wait(barrier, count)


def gather_kernel(dims, rows_a, shard_ref, img_ref, out_ref, img_out, own_sem, img_sems, send_sems, recv_sems, core_send, core_recv):
    size_z, size_y, size_x = dims
    s = lax.axis_index("section")
    z, y, x = place(dims)
    rows = shard_ref.shape[0]
    part_a, part_b = pl.ds(0, rows_a), pl.ds(rows_a, rows - rows_a)
    greet(dims, s, z, y, x)
    mine = out_ref.at[s]
    waiting = []
    counter = [0, 0]

    def remote(src, dst, there):
        slot = counter[0]
        counter[0] += 1
        copy = pltpu.make_async_remote_copy(
            src_ref=src, dst_ref=dst, send_sem=send_sems.at[slot], recv_sem=recv_sems.at[slot],
            device_id={"dp": rank(dims, *there)}, device_id_type=MESH,
        )
        copy.start()
        waiting.append(copy)
        return copy

    arriving = []

    def to_core(piece, other):
        slot = counter[1]
        counter[1] += 1
        copy = pltpu.make_async_remote_copy(
            src_ref=piece, dst_ref=piece, send_sem=core_send.at[slot], recv_sem=core_recv.at[slot],
            device_id={"section": 1 - s}, device_id_type=MESH,
        )
        copy.start()
        waiting.append(copy)
        arriving.append(pltpu.make_async_remote_copy(
            src_ref=other, dst_ref=other, send_sem=core_send.at[slot], recv_sem=core_recv.at[slot],
            device_id={"section": 1 - s}, device_id_type=MESH,
        ))

    def block(section, at_z, at_y, at_x, part):
        return out_ref.at[section, at_z, at_y, at_x, part]

    image = pltpu.make_async_remote_copy(
        src_ref=img_ref.at[1 - s], dst_ref=img_out, send_sem=img_sems.at[0], recv_sem=img_sems.at[1],
        device_id={"section": 1 - s}, device_id_type=MESH,
    )
    image.start()
    every = slice(None)
    whole = pl.ds(0, rows)
    first = [
        (remote(shard_ref, mine.at[z, y, x], ((z + d) % size_z, y, x)), (z - d + size_z) % size_z)
        for d in range(1, size_z)
    ]
    own = pltpu.make_async_copy(shard_ref, mine.at[z, y, x], own_sem)
    own.start()
    own.wait()
    to_core(block(s, z, y, x, whole), block(1 - s, z, y, x, whole))
    for copy, from_z in first:
        copy.wait_recv()
        to_core(block(s, from_z, y, x, whole), block(1 - s, from_z, y, x, whole))

    second = []
    for d in range(1, size_y):
        piece = block(s, every, y, x, part_a)
        second.append((remote(piece, piece, (z, (y + d) % size_y, x)), 0, (y - d + size_y) % size_y))
    for d in range(1, size_x):
        piece = block(s, every, y, x, part_b)
        second.append((remote(piece, piece, (z, y, (x + d) % size_x)), 1, (x - d + size_x) % size_x))
    for copy, kind, at in second:
        copy.wait_recv()
        if kind == 0:
            to_core(block(s, every, at, x, part_a), block(1 - s, every, at, x, part_a))
        else:
            to_core(block(s, every, y, at, part_b), block(1 - s, every, y, at, part_b))

    third = []
    for d in range(1, size_x):
        piece = block(s, every, every, x, part_a)
        third.append((remote(piece, piece, (z, y, (x + d) % size_x)), 0, (x - d + size_x) % size_x))
    for d in range(1, size_y):
        piece = block(s, every, y, every, part_b)
        third.append((remote(piece, piece, (z, (y + d) % size_y, x)), 1, (y - d + size_y) % size_y))
    for copy, kind, at in third:
        copy.wait_recv()
        if kind == 0:
            to_core(block(s, every, every, at, part_a), block(1 - s, every, every, at, part_a))
        else:
            to_core(block(s, every, at, every, part_b), block(1 - s, every, at, every, part_b))
    for copy in waiting:
        copy.wait_send()
    for copy in arriving:
        copy.wait_recv()
    image.wait()


def gather(dims, shard, images):
    rows, width = shard.shape
    rows_a = 16 * (rows // 32)
    size_z, size_y, size_x = dims
    across = (size_z - 1) + 2 * (size_y - 1) + 2 * (size_x - 1)
    any_spec = pl.BlockSpec(memory_space=pl.ANY)
    return pl.pallas_call(
        functools.partial(gather_kernel, dims, rows_a),
        out_shape=(
            jax.ShapeDtypeStruct((2,) + dims + (rows, width), bf16),
            jax.ShapeDtypeStruct(images.shape[1:], bf16),
        ),
        in_specs=[any_spec] * 2,
        out_specs=(any_spec, any_spec),
        scratch_shapes=[
            pltpu.SemaphoreType.DMA,
            pltpu.SemaphoreType.DMA((2,)),
            pltpu.SemaphoreType.DMA((max(across, 1),)),
            pltpu.SemaphoreType.DMA((max(across, 1),)),
            pltpu.SemaphoreType.DMA((across + 1,)),
            pltpu.SemaphoreType.DMA((across + 1,)),
        ],
        compiler_params=pltpu.CompilerParams(collective_id=0, has_side_effects=True, vmem_limit_bytes=VMEM_BYTES),
        name="weight_gather",
    )(shard, images)


def scatter_kernel(dims, rows_a, part_ref, rows_ref, out_ref, rows_out, core_in, work, in_one_a, in_one_b,
                   two_a, two_b, in_two_a, in_two_b, three, in_three, row_sems, send_sems, recv_sems, core_send, core_recv):
    size_z, size_y, size_x = dims
    s = lax.axis_index("section")
    z, y, x = place(dims)
    rows = out_ref.shape[0]
    part_a, part_b = pl.ds(0, rows_a), pl.ds(rows_a, rows - rows_a)
    every = slice(None)
    greet(dims, s, z, y, x)
    waiting = []
    counter = [0]

    def remote(src, dst, there):
        slot = counter[0]
        counter[0] += 1
        copy = pltpu.make_async_remote_copy(
            src_ref=src, dst_ref=dst, send_sem=send_sems.at[slot], recv_sem=recv_sems.at[slot],
            device_id={"dp": rank(dims, *there)}, device_id_type=MESH,
        )
        copy.start()
        waiting.append(copy)
        return copy

    chunks = []
    for d in list(range(1, max(size_x, size_y))) + [0]:
        if d < size_x:
            chunks.append((0, d, (x + d) % size_x))
        if d < size_y:
            chunks.append((1, d, (y + d) % size_y))
    cores = []
    for slot, (kind, d, at) in enumerate(chunks):
        if kind == 0:
            src, dst = part_ref.at[1 - s, :, :, at, part_a], core_in.at[:, :, at, part_a]
        else:
            src, dst = part_ref.at[1 - s, :, at, :, part_b], core_in.at[:, at, :, part_b]
        copy = pltpu.make_async_remote_copy(
            src_ref=src, dst_ref=dst, send_sem=core_send.at[slot], recv_sem=core_recv.at[slot],
            device_id={"section": 1 - s}, device_id_type=MESH,
        )
        copy.start()
        cores.append(copy)
    row_copy = pltpu.make_async_remote_copy(
        src_ref=rows_ref.at[s], dst_ref=rows_out, send_sem=row_sems.at[0], recv_sem=row_sems.at[1],
        device_id={"section": 1 - s}, device_id_type=MESH,
    )
    row_copy.start()

    one_a, one_b = [], []
    for copy, (kind, d, at) in zip(cores, chunks):
        copy.wait_recv()
        if kind == 0:
            @pl.loop(0, size_z * size_y)
            def _(i):
                u, v = i // size_y, i % size_y
                work[u, v, at, part_a] = (
                    part_ref[s, u, v, at, part_a].astype(f32) + core_in[u, v, at, part_a].astype(f32)
                ).astype(bf16)
            if d:
                one_a.append(remote(work.at[:, :, at, part_a], in_one_a.at[d - 1], (z, y, at)))
        else:
            @pl.loop(0, size_z * size_x)
            def _(i):
                u, v = i // size_x, i % size_x
                work[u, at, v, part_b] = (
                    part_ref[s, u, at, v, part_b].astype(f32) + core_in[u, at, v, part_b].astype(f32)
                ).astype(bf16)
            if d:
                one_b.append(remote(work.at[:, at, :, part_b], in_one_b.at[d - 1], (z, at, x)))

    for copy in one_a:
        copy.wait_recv()

    @pl.loop(0, size_z * size_y)
    def _(i):
        u, v = i // size_y, i % size_y
        total = work[u, v, x, part_a].astype(f32)
        for d in range(1, size_x):
            total = total + in_one_a[d - 1, u, v].astype(f32)
        two_a[v, u] = total.astype(bf16)

    go_a = [remote(two_a.at[(y + d) % size_y], in_two_a.at[d - 1], (z, (y + d) % size_y, x)) for d in range(1, size_y)]
    for copy in one_b:
        copy.wait_recv()

    @pl.loop(0, size_z * size_x)
    def _(i):
        u, v = i // size_x, i % size_x
        total = work[u, y, v, part_b].astype(f32)
        for d in range(1, size_y):
            total = total + in_one_b[d - 1, u, v].astype(f32)
        two_b[v, u] = total.astype(bf16)

    go_b = [remote(two_b.at[(x + d) % size_x], in_two_b.at[d - 1], (z, y, (x + d) % size_x)) for d in range(1, size_x)]
    for copy in go_a + go_b:
        copy.wait_recv()

    @pl.loop(0, size_z)
    def _(u):
        total = two_a[y, u].astype(f32)
        for d in range(1, size_y):
            total = total + in_two_a[d - 1, u].astype(f32)
        three[u, part_a] = total.astype(bf16)
        total = two_b[x, u].astype(f32)
        for d in range(1, size_x):
            total = total + in_two_b[d - 1, u].astype(f32)
        three[u, part_b] = total.astype(bf16)

    last = [remote(three.at[(z + d) % size_z], in_three.at[d - 1], ((z + d) % size_z, y, x)) for d in range(1, size_z)]
    for copy in last:
        copy.wait_recv()
    total = three[z].astype(f32)
    for d in range(1, size_z):
        total = total + in_three[d - 1].astype(f32)
    out_ref[...] = total
    for copy in waiting + cores:
        copy.wait_send()
    row_copy.wait()


def scatter(dims, partials, rows_pair):
    rows, width = partials.shape[-2:]
    rows_a = 16 * (rows // 32)
    rows_b = rows - rows_a
    size_z, size_y, size_x = dims
    across = (size_z - 1) + 2 * (size_y - 1) + 2 * (size_x - 1)
    vmem = pl.BlockSpec(memory_space=pltpu.VMEM)
    any_spec = pl.BlockSpec(memory_space=pl.ANY)
    more = lambda size: max(size - 1, 1)
    return pl.pallas_call(
        functools.partial(scatter_kernel, dims, rows_a),
        out_shape=(
            jax.ShapeDtypeStruct((rows, width), f32),
            jax.ShapeDtypeStruct(rows_pair.shape[1:], bf16),
        ),
        in_specs=[vmem, any_spec],
        out_specs=(vmem, any_spec),
        scratch_shapes=[
            pltpu.VMEM(dims + (rows, width), bf16),
            pltpu.VMEM(dims + (rows, width), bf16),
            pltpu.VMEM((more(size_x), size_z, size_y, rows_a, width), bf16),
            pltpu.VMEM((more(size_y), size_z, size_x, rows_b, width), bf16),
            pltpu.VMEM((size_y, size_z, rows_a, width), bf16),
            pltpu.VMEM((size_x, size_z, rows_b, width), bf16),
            pltpu.VMEM((more(size_y), size_z, rows_a, width), bf16),
            pltpu.VMEM((more(size_x), size_z, rows_b, width), bf16),
            pltpu.VMEM((size_z, rows, width), bf16),
            pltpu.VMEM((more(size_z), rows, width), bf16),
            pltpu.SemaphoreType.DMA((2,)),
            pltpu.SemaphoreType.DMA((max(across, 1),)),
            pltpu.SemaphoreType.DMA((max(across, 1),)),
            pltpu.SemaphoreType.DMA((size_x + size_y,)),
            pltpu.SemaphoreType.DMA((size_x + size_y,)),
        ],
        compiler_params=pltpu.CompilerParams(collective_id=1, has_side_effects=True, vmem_limit_bytes=VMEM_BYTES),
        name="grad_scatter",
    )(partials, rows_pair)


def mm(left, right):
    return jnp.dot(left, right, preferred_element_type=f32)


def mm_t(left, right):
    return lax.dot_general(left, right, (((1,), (1,)), ((), ())), preferred_element_type=f32)


def t_mm(left, right):
    return lax.dot_general(left, right, (((0,), (0,)), ((), ())), preferred_element_type=f32)


def norm_parts(values):
    average = jnp.mean(values, axis=-1, keepdims=True)
    centered = values - average
    inverse = lax.rsqrt(jnp.mean(centered * centered, axis=-1, keepdims=True) + EPS)
    return centered * inverse, inverse


def norm_back(unit, inverse, gain, grad):
    scaled = grad * (1.0 + gain)
    mean_one = jnp.mean(scaled, axis=-1, keepdims=True)
    mean_two = jnp.mean(scaled * unit, axis=-1, keepdims=True)
    return (
        inverse * (scaled - mean_one - unit * mean_two),
        jnp.sum(grad * unit, axis=0, keepdims=True),
        jnp.sum(grad, axis=0, keepdims=True),
    )


def layers_kernel(seq, rows_ref, cot_ref, vec_ref, bias_ref, qkv_ref, wo_ref, up_ref, down_ref,
                  y_ref, dh_ref, gvec_ref, gbias_ref, gqkv_ref, gwo_ref, gup_ref, gdown_ref,
                  h_s, a_s, q_s, o_s, z_s, n_s, g_s, slope_s, pf_s, dn_s, dy_s, dqkv_s):
    rows, width = cot_ref.shape
    ff = up_ref.shape[-1]
    pairs = width // PAIR
    lane = lax.broadcasted_iota(jnp.int32, (rows, PAIR), 1)
    low_half = lane < HEAD_DIM
    key_ok = lax.broadcasted_iota(jnp.int32, (rows, rows), 1) < seq
    zero = jnp.zeros((rows, PAIR), bf16)

    def halves(values):
        return jnp.where(low_half, values, zero), jnp.where(low_half, zero, values)

    h_s[0] = rows_ref[...].astype(f32)

    @pl.loop(0, 2)
    def _(e):
        vec = vec_ref[e]
        h = h_s[e]
        unit, _ = norm_parts(h)
        a = (unit * (1.0 + vec[0:1]) + vec[1:2]).astype(bf16)
        a_s[e] = a
        for third in range(3):
            cols = slice(third * width, (third + 1) * width)
            part = mm(a, qkv_ref[e, :, cols])
            if third != 1:
                part = part + vec[2 + third // 2:3 + third // 2]
            q_s[e, :, cols] = part.astype(bf16)
        for j in range(pairs):
            q = q_s[e, :, j * PAIR:(j + 1) * PAIR]
            k = q_s[e, :, width + j * PAIR:width + (j + 1) * PAIR]
            v = q_s[e, :, 2 * width + j * PAIR:2 * width + (j + 1) * PAIR]
            outs = []
            for i, q_half in enumerate(halves(q)):
                scores = jnp.where(key_ok, mm_t(q_half, k) * SCALE, -1e30)
                shifted = jnp.exp(scores - jnp.max(scores, axis=-1, keepdims=True))
                pf = shifted / jnp.sum(shifted, axis=-1, keepdims=True)
                pf_s[e, 2 * j + i] = pf
                outs.append(mm(pf.astype(bf16), v))
            o_s[e, :, j * PAIR:(j + 1) * PAIR] = jnp.where(low_half, outs[0], outs[1]).astype(bf16)
        z = h + mm(o_s[e], wo_ref[e]) + vec[4:5]
        z_s[e] = z
        unit, _ = norm_parts(z)
        n = (unit * (1.0 + vec[5:6]) + vec[6:7]).astype(bf16)
        n_s[e] = n
        for c in range(ff // width):
            cols = slice(c * width, (c + 1) * width)
            u = mm(n, up_ref[e, :, cols]) + bias_ref[e, :, cols]
            phi = 0.5 + 0.5 * lax.erf(u * (0.5 ** 0.5))
            g_s[e, :, cols] = (u * phi).astype(bf16)
            slope_s[e, :, cols] = phi + u * (jnp.exp(-0.5 * u * u) * 0.3989422804014327)
        result = (z + mm(g_s[e], down_ref[e]) + vec[7:8]).astype(bf16)
        y_ref[...] = result
        h_s[1] = jnp.where(e == 0, result.astype(f32), h_s[1])

    dy_s[...] = cot_ref[...].astype(f32)

    @pl.loop(0, 2)
    def _(step):
        e = 1 - step
        vec = vec_ref[e]
        dy = dy_s[...]
        dm = dy.astype(bf16)
        g7 = jnp.sum(dm.astype(f32), axis=0, keepdims=True)
        n = n_s[e]
        for c in range(ff // width):
            cols = slice(c * width, (c + 1) * width)
            gdown_ref[e, cols, :] = t_mm(g_s[e, :, cols], dm).astype(bf16)
            du = (mm_t(dm, down_ref[e, cols, :]) * slope_s[e, :, cols]).astype(bf16)
            gbias_ref[e, :, cols] = jnp.sum(du.astype(f32), axis=0, keepdims=True)
            gup_ref[e, :, cols] = t_mm(n, du).astype(bf16)
            back = mm_t(du, up_ref[e, :, cols])
            if c == 0:
                dn_s[...] = back
            else:
                dn_s[...] += back
        unit, inverse = norm_parts(z_s[e])
        dz, g5, g6 = norm_back(unit, inverse, vec[5:6], dn_s[...])
        dz = dz + dy
        dr = dz.astype(bf16)
        g4 = jnp.sum(dr.astype(f32), axis=0, keepdims=True)
        gwo_ref[e] = t_mm(o_s[e], dr).astype(bf16)
        do_all = mm_t(dr, wo_ref[e]).astype(bf16)
        for j in range(pairs):
            q = q_s[e, :, j * PAIR:(j + 1) * PAIR]
            k = q_s[e, :, width + j * PAIR:width + (j + 1) * PAIR]
            v = q_s[e, :, 2 * width + j * PAIR:2 * width + (j + 1) * PAIR]
            do = do_all[:, j * PAIR:(j + 1) * PAIR]
            dq, dk, dv = [], [], []
            for i, do_half in enumerate(halves(do)):
                pf = pf_s[e, 2 * j + i]
                dp = mm_t(do_half, v)
                ds = (pf * (dp - jnp.sum(pf * dp, axis=-1, keepdims=True))).astype(bf16)
                dv.append(t_mm(pf.astype(bf16), do))
                dq.append(mm(ds, k))
                dk.append(t_mm(ds, q))
            dqkv_s[:, j * PAIR:(j + 1) * PAIR] = (jnp.where(low_half, dq[0], dq[1]) * SCALE).astype(bf16)
            dqkv_s[:, width + j * PAIR:width + (j + 1) * PAIR] = (jnp.where(low_half, dk[0], dk[1]) * SCALE).astype(bf16)
            dqkv_s[:, 2 * width + j * PAIR:2 * width + (j + 1) * PAIR] = jnp.where(low_half, dv[0], dv[1]).astype(bf16)
        a = a_s[e]
        sums = []
        for third in range(3):
            cols = slice(third * width, (third + 1) * width)
            dpart = dqkv_s[:, cols]
            sums.append(jnp.sum(dpart.astype(f32), axis=0, keepdims=True))
            gqkv_ref[e, :, cols] = t_mm(a, dpart).astype(bf16)
            back = mm_t(dpart, qkv_ref[e, :, cols])
            if third == 0:
                dn_s[...] = back
            else:
                dn_s[...] += back
        unit, inverse = norm_parts(h_s[e])
        dh, g0, g1 = norm_back(unit, inverse, vec[0:1], dn_s[...])
        low = (dz + dh).astype(bf16)
        dh_ref[...] = low
        dy_s[...] = low.astype(f32)
        for row, value in enumerate((g0, g1, sums[0], sums[2], g4, g5, g6, g7)):
            gvec_ref[e, row:row + 1, :] = value


def run_layers(seq, rows, cot, vec, bias, qkv, wo, up, down):
    t, width = rows.shape
    ff = up.shape[-1]
    vmem = pl.BlockSpec(memory_space=pltpu.VMEM)
    shape = jax.ShapeDtypeStruct
    return pl.pallas_call(
        functools.partial(layers_kernel, seq),
        out_shape=(
            shape((t, width), bf16), shape((t, width), bf16), shape(vec.shape, f32), shape(bias.shape, f32),
            shape(qkv.shape, bf16), shape(wo.shape, bf16), shape(up.shape, bf16), shape(down.shape, bf16),
        ),
        in_specs=[vmem] * 8,
        out_specs=(vmem,) * 8,
        scratch_shapes=[
            pltpu.VMEM((2, t, width), f32),
            pltpu.VMEM((2, t, width), bf16),
            pltpu.VMEM((2, t, 3 * width), bf16),
            pltpu.VMEM((2, t, width), bf16),
            pltpu.VMEM((2, t, width), f32),
            pltpu.VMEM((2, t, width), bf16),
            pltpu.VMEM((2, t, ff), bf16),
            pltpu.VMEM((2, t, ff), f32),
            pltpu.VMEM((2, HEADS, t, t), f32),
            pltpu.VMEM((t, width), f32),
            pltpu.VMEM((t, width), f32),
            pltpu.VMEM((t, 3 * width), bf16),
        ],
        compiler_params=pltpu.CompilerParams(vmem_limit_bytes=VMEM_BYTES),
        name="two_layers",
    )(rows, cot, vec, bias, qkv, wo, up, down)


def split_cols(matrix, count, width):
    lead, (tall, wide) = matrix.shape[:-2], matrix.shape[-2:]
    per, across = tall // count, wide // width
    blocks = jnp.swapaxes(matrix.reshape(lead + (count, per, across, width)), -3, -2)
    return blocks.reshape(lead + (count, across * per, width))


def join_cols(blocks, per, width):
    lead, (count, tall) = blocks.shape[:-3], blocks.shape[-3:-1]
    across = tall // per
    matrix = jnp.swapaxes(blocks.reshape(lead + (count, across, per, width)), -3, -2)
    return matrix.reshape(lead + (count * per, across * width))


def pack(count, width, small, qkv, wo, up, down):
    lead = small.shape[:-2]
    pieces = [split_cols(m, count, width) for m in (qkv, wo, up, down)]
    used = sum(piece.shape[-2] for piece in pieces)
    small_rows = -(-small.shape[-1] // width)
    rows = -(-(used + small_rows) // 16) * 16
    room = (rows - used) * width
    padded = jnp.pad(small, [(0, 0)] * (small.ndim - 1) + [(0, room - small.shape[-1])])
    pieces.append(padded.reshape(lead + (count, rows - used, width)))
    return jnp.concatenate(pieces, axis=-2)


def unpack(blocks, per, ff_per, ff, vec_rows):
    width = blocks.shape[-1]
    ends = [3 * per, 4 * per, 4 * per + (ff // width) * per]
    ends.append(ends[-1] + ff_per)
    qkv = join_cols(blocks[..., :ends[0], :], per, width)
    wo = join_cols(blocks[..., ends[0]:ends[1], :], per, width)
    up = join_cols(blocks[..., ends[1]:ends[2], :], per, width)
    down = join_cols(blocks[..., ends[2]:ends[3], :], ff_per, width)
    tail = blocks[..., ends[3]:, :]
    small = tail.reshape(tail.shape[:-2] + (-1,))
    vec = small[..., :vec_rows * per].reshape(small.shape[:-1] + (vec_rows, per))
    vec = jnp.moveaxis(vec, -2, -3)
    vec = vec.reshape(vec.shape[:-2] + (-1,))
    bias = small[..., vec_rows * per:vec_rows * per + ff_per]
    bias = bias.reshape(bias.shape[:-2] + (-1,))
    return vec, bias, qkv, wo, up, down


def shards(dims, ends_in, vectors, up_bias, w_qkv, w_out, w_up, w_down):
    section_id = lax.axis_index("section")
    is_first = section_id == 0
    local = ends_in[0]
    _, seq, width = local.shape
    count = dims[0] * dims[1] * dims[2]
    vec_rows, per = vectors.shape[1:]
    ff_per = up_bias.shape[1]
    ff = ff_per * count
    t = -(-seq // 16) * 16
    padded = jnp.pad(local, ((0, 0), (0, t - seq), (0, 0)))
    small = jnp.concatenate([vectors[0].reshape(1, -1), up_bias], axis=-1)
    shard = pack(1, width, small, w_qkv[0], w_out[0], w_up[0], w_down[0])[0]
    blocks, other = gather(dims, shard, padded)
    vec, bias, qkv, wo, up, down = unpack(blocks.reshape((2, count) + shard.shape), per, ff_per, ff, vec_rows)
    own = lax.dynamic_index_in_dim(padded, section_id, 0, keepdims=False)
    rows = jnp.where(is_first, own, other)
    cot = jnp.where(is_first, other, own)
    y, dh, gvec, gbias, gqkv, gwo, gup, gdown = run_layers(
        seq, rows, cot, vec.astype(f32), bias.astype(f32)[:, None], qkv, wo, up, down
    )
    gvec = jnp.moveaxis(gvec.reshape(2, vec_rows, count, per), 2, 1).reshape(2, count, vec_rows * per)
    gsmall = jnp.concatenate([gvec, gbias.reshape(2, count, ff_per)], axis=-1).astype(bf16)
    partials = pack(count, width, gsmall, gqkv, gwo, gup, gdown)
    total, got = scatter(dims, partials.reshape((2,) + dims + partials.shape[-2:]), jnp.stack([y, dh]))
    fvec, fbias, fqkv, fwo, fup, fdown = unpack(total[None], per, ff_per, ff, vec_rows)
    ends = jnp.stack([jnp.where(is_first, dh, got), jnp.where(is_first, got, y)])[None, :, :seq]
    return ends, fvec[None], fbias[None], fqkv[None], fwo[None], fup[None], fdown[None]


def solution(mesh):
    dims = chip_grid(mesh.shape["dp"])
    specs = (
        P("section", "dp", None, None),
        P("section", None, "dp"),
        P("section", "dp"),
        P("section", "dp", None),
        P("section", "dp", None),
        P("section", "dp", None),
        P("section", "dp", None),
    )
    return jax.shard_map(
        functools.partial(shards, dims), mesh=mesh, in_specs=specs, out_specs=specs, check_vma=False
    )
```

```python
import functools

import jax
import jax.numpy as jnp
from jax import lax
from jax.experimental import pallas as pl
from jax.experimental.pallas import tpu as pltpu
from jax.sharding import PartitionSpec as P

HEADS = 6
HEAD_DIM = 64
PAIR = 2 * HEAD_DIM
EPS = 1e-06
SCALE = HEAD_DIM ** (-0.5)
CHUNKS = 4
VMEM_BYTES = 56 * 1024 * 1024

bf16 = jnp.bfloat16
f32 = jnp.float32
MESH = pl.DeviceIdType.MESH


def chip_grid(count):
    for side in range(1, count + 1):
        if 2 * side**3 == count:
            return (2 * side, side, side)
    return (count, 1, 1)


def place(dims):
    me = lax.axis_index("dp")
    _, size_y, size_x = dims
    return me // (size_y * size_x), (me // size_x) % size_y, me % size_x


def rank(dims, z, y, x):
    return (z * dims[1] + y) * dims[2] + x


def greet(dims, s, z, y, x):
    barrier = pltpu.get_barrier_semaphore()
    count = 1
    pl.semaphore_signal(barrier, inc=1, device_id={"section": 1 - s}, device_id_type=MESH)
    for axis, (size, at) in enumerate(zip(dims, (z, y, x))):
        for d in range(1, size):
            there = [z, y, x]
            there[axis] = (at + d) % size
            pl.semaphore_signal(barrier, inc=1, device_id={"dp": rank(dims, *there)}, device_id_type=MESH)
            count += 1
    pl.semaphore_wait(barrier, count)


def row_chunks(rows):
    tiles = rows // 16
    parts = min(CHUNKS, tiles)
    cuts = [16 * (tiles * i // parts) for i in range(parts + 1)]
    return [(low, high - low) for low, high in zip(cuts, cuts[1:])]


def selector(tall, wide, offset):
    row = lax.broadcasted_iota(jnp.int32, (tall, wide), 0)
    col = lax.broadcasted_iota(jnp.int32, (tall, wide), 1)
    return jnp.where(col == row + offset, 1.0, 0.0).astype(f32)


def build_shard(dims, vec_ref, bias_ref, qkv_ref, wo_ref, up_ref, down_ref, shard):
    per, width = wo_ref.shape
    ff_per = down_ref.shape[0]
    me = lax.axis_index("dp")
    ups = up_ref.shape[1] // width
    pieces = [qkv_ref[:, i * width:(i + 1) * width] for i in range(3)] + [wo_ref[...]]
    pieces += [up_ref[:, i * width:(i + 1) * width] for i in range(ups)]
    for i in range(0, len(pieces), 2):
        both = jnp.concatenate([pieces[i].astype(f32), pieces[i + 1].astype(f32)], axis=0)
        shard[i * per:(i + 2) * per] = both.astype(bf16)
    top = len(pieces) * per
    shard[top:top + ff_per] = down_ref[...]
    shard[top + ff_per:] = build_tail(me, vec_ref[...], bias_ref[...], ups, width).astype(bf16)


def build_tail(me, vec, bias, ups, width):
    per, ff_per = vec.shape[1], bias.shape[1]
    put = jnp.dot(vec.astype(f32), selector(per, width, me * per), preferred_element_type=f32)
    line = jnp.dot(jnp.broadcast_to(bias.astype(f32), (8, ff_per)), selector(ff_per, width, (me * ff_per) % width),
                   preferred_element_type=f32)
    at = lax.broadcasted_iota(jnp.int32, (8, width), 0)
    return jnp.concatenate([put, jnp.where(at == (me * ff_per) // width, line, 0.0)], axis=0)


def gather_kernel(dims, fast, *refs):
    if fast:
        vec_ref, bias_ref, qkv_ref, wo_ref, up_ref, down_ref, img_ref, out_ref, img_out, shard_ref = refs[:10]
    else:
        shard_ref, img_ref, out_ref, img_out = refs[:4]
    own_sem, img_sems, send_sems, recv_sems, core_send, core_recv = refs[-6:]
    size_z, side, _ = dims
    s = lax.axis_index("section")
    z, y, x = place(dims)
    if fast:
        build_shard(dims, vec_ref, bias_ref, qkv_ref, wo_ref, up_ref, down_ref, shard_ref)
    rows = shard_ref.shape[0]
    greet(dims, s, z, y, x)
    waiting = []
    arriving = []
    counter = [0, 0]

    def remote(src, dst, there):
        slot = counter[0]
        counter[0] += 1
        copy = pltpu.make_async_remote_copy(
            src_ref=src, dst_ref=dst, send_sem=send_sems.at[slot], recv_sem=recv_sems.at[slot],
            device_id={"dp": rank(dims, *there)}, device_id_type=MESH,
        )
        copy.start()
        waiting.append(copy)
        return copy

    def to_core(*at):
        slot = counter[1]
        counter[1] += 1
        for section, do_start in ((s, True), (1 - s, False)):
            piece = out_ref.at[(section,) + at]
            copy = pltpu.make_async_remote_copy(
                src_ref=piece, dst_ref=piece, send_sem=core_send.at[slot], recv_sem=core_recv.at[slot],
                device_id={"section": 1 - s}, device_id_type=MESH,
            )
            if do_start:
                copy.start()
                waiting.append(copy)
            else:
                arriving.append(copy)

    image = pltpu.make_async_remote_copy(
        src_ref=img_ref.at[1 - s], dst_ref=img_out, send_sem=img_sems.at[0], recv_sem=img_sems.at[1],
        device_id={"section": 1 - s}, device_id_type=MESH,
    )
    every = slice(None)
    chunks = [pl.ds(low, size) for low, size in row_chunks(rows)]
    first = []
    for part in chunks:
        first.append([
            (remote(shard_ref.at[part], out_ref.at[s, z, y, x, part], ((z + d) % size_z, y, x)), (z - d + size_z) % size_z)
            for d in range(1, size_z)
        ])
    own = pltpu.make_async_copy(shard_ref, out_ref.at[s, z, y, x], own_sem)
    own.start()
    image.start()
    own.wait()
    to_core(z, y, x)

    second, third = {}, {}
    for t in range(len(chunks) + 2):
        if t < len(chunks):
            part = chunks[t]
            for copy, from_z in first[t]:
                copy.wait_recv()
                to_core(from_z, y, x, part)
            piece = out_ref.at[s, every, y, x, part]
            second[t] = []
            for d in range(1, side):
                if t % 2 == 0:
                    second[t].append((remote(piece, piece, (z, (y + d) % side, x)), (y - d + side) % side))
                else:
                    second[t].append((remote(piece, piece, (z, y, (x + d) % side)), (x - d + side) % side))
        c = t - 1
        if 0 <= c < len(chunks):
            part = chunks[c]
            for copy, at in second[c]:
                copy.wait_recv()
                if c % 2 == 0:
                    to_core(every, at, x, part)
                else:
                    to_core(every, y, at, part)
            third[c] = []
            for d in range(1, side):
                if c % 2 == 0:
                    piece = out_ref.at[s, every, every, x, part]
                    third[c].append((remote(piece, piece, (z, y, (x + d) % side)), (x - d + side) % side))
                else:
                    piece = out_ref.at[s, every, y, every, part]
                    third[c].append((remote(piece, piece, (z, (y + d) % side, x)), (y - d + side) % side))
        c = t - 2
        if 0 <= c < len(chunks):
            part = chunks[c]
            for copy, at in third[c]:
                copy.wait_recv()
                if c % 2 == 0:
                    to_core(every, every, at, part)
                else:
                    to_core(every, at, every, part)
    for copy in waiting:
        copy.wait_send()
    for copy in arriving:
        copy.wait_recv()
    image.wait()


def gather(dims, fast, sources, images, rows, width):
    size_z, side, _ = dims
    parts = len(row_chunks(rows))
    across = parts * ((size_z - 1) + 2 * (side - 1))
    any_spec = pl.BlockSpec(memory_space=pl.ANY)
    vmem = pl.BlockSpec(memory_space=pltpu.VMEM)
    sems = [
        pltpu.SemaphoreType.DMA,
        pltpu.SemaphoreType.DMA((2,)),
        pltpu.SemaphoreType.DMA((max(across, 1),)),
        pltpu.SemaphoreType.DMA((max(across, 1),)),
        pltpu.SemaphoreType.DMA((across + 1,)),
        pltpu.SemaphoreType.DMA((across + 1,)),
    ]
    return pl.pallas_call(
        functools.partial(gather_kernel, dims, fast),
        out_shape=(
            jax.ShapeDtypeStruct((2,) + dims + (rows, width), bf16),
            jax.ShapeDtypeStruct(images.shape[1:], bf16),
        ),
        in_specs=[vmem] * len(sources) + [any_spec] if fast else [any_spec] * 2,
        out_specs=(any_spec, any_spec),
        scratch_shapes=([pltpu.VMEM((rows, width), bf16)] if fast else []) + sems,
        compiler_params=pltpu.CompilerParams(collective_id=0, has_side_effects=True, vmem_limit_bytes=VMEM_BYTES),
        name="weight_gather",
    )(*sources, images)


def scatter_kernel(dims, part_ref, rows_ref, *refs):
    outs, rows_out = refs[:-14], refs[-14]
    (core_in, work, in_one, two, in_two, three, in_three, total_s,
     row_sems, send_sems, recv_sems, core_send, core_recv) = refs[-13:]
    size_z, side, _ = dims
    s = lax.axis_index("section")
    z, y, x = place(dims)
    rows = total_s.shape[0]
    every = slice(None)
    greet(dims, s, z, y, x)
    waiting = []
    counter = [0]

    def remote(src, dst, there):
        slot = counter[0]
        counter[0] += 1
        copy = pltpu.make_async_remote_copy(
            src_ref=src, dst_ref=dst, send_sem=send_sems.at[slot], recv_sem=recv_sems.at[slot],
            device_id={"dp": rank(dims, *there)}, device_id_type=MESH,
        )
        copy.start()
        waiting.append(copy)
        return copy

    chunks = [pl.ds(low, size) for low, size in row_chunks(rows)]
    cores = []
    for slot, part in enumerate(chunks):
        copy = pltpu.make_async_remote_copy(
            src_ref=part_ref.at[1 - s, :, :, :, part], dst_ref=core_in.at[:, :, :, part],
            send_sem=core_send.at[slot], recv_sem=core_recv.at[slot],
            device_id={"section": 1 - s}, device_id_type=MESH,
        )
        copy.start()
        cores.append(copy)
    row_copy = pltpu.make_async_remote_copy(
        src_ref=rows_ref.at[s], dst_ref=rows_out, send_sem=row_sems.at[0], recv_sem=row_sems.at[1],
        device_id={"section": 1 - s}, device_id_type=MESH,
    )
    row_copy.start()

    def step_core(c):
        part = chunks[c]
        cores[c].wait_recv()

        @pl.loop(0, size_z * side * side)
        def _(i):
            u, v, w = i // (side * side), (i // side) % side, i % side
            work[u, v, w, part] = (part_ref[s, u, v, w, part].astype(f32) + core_in[u, v, w, part].astype(f32)).astype(bf16)

        sent = []
        for d in range(1, side):
            if c % 2 == 0:
                at = (x + d) % side
                sent.append(remote(work.at[:, :, at, part], in_one.at[d - 1, :, :, part], (z, y, at)))
            else:
                at = (y + d) % side
                sent.append(remote(work.at[:, at, :, part], in_one.at[d - 1, :, :, part], (z, at, x)))
        return sent

    def step_one(c, sent):
        part = chunks[c]
        for copy in sent:
            copy.wait_recv()

        @pl.loop(0, size_z * side)
        def _(i):
            u, v = i // side, i % side
            at = (u, v, x) if c % 2 == 0 else (u, y, v)
            total = work[at + (part,)].astype(f32)
            for d in range(1, side):
                total = total + in_one[d - 1, u, v, part].astype(f32)
            two[v, u, part] = total.astype(bf16)

        sent = []
        for d in range(1, side):
            at = ((y if c % 2 == 0 else x) + d) % side
            there = (z, at, x) if c % 2 == 0 else (z, y, at)
            sent.append(remote(two.at[at, :, part], in_two.at[d - 1, :, part], there))
        return sent

    def step_two(c, sent):
        part = chunks[c]
        for copy in sent:
            copy.wait_recv()

        @pl.loop(0, size_z)
        def _(u):
            total = two[y if c % 2 == 0 else x, u, part].astype(f32)
            for d in range(1, side):
                total = total + in_two[d - 1, u, part].astype(f32)
            three[u, part] = total.astype(bf16)

        return [
            remote(three.at[(z + d) % size_z, part], in_three.at[d - 1, part], ((z + d) % size_z, y, x))
            for d in range(1, size_z)
        ]

    def step_three(c, sent):
        part = chunks[c]
        for copy in sent:
            copy.wait_recv()
        total = three[z, part].astype(f32)
        for d in range(1, size_z):
            total = total + in_three[d - 1, part].astype(f32)
        total_s[part] = total

    one, again, last = {}, {}, {}
    for t in range(len(chunks) + 3):
        if t < len(chunks):
            one[t] = step_core(t)
        if 0 <= t - 1 < len(chunks):
            again[t - 1] = step_one(t - 1, one[t - 1])
        if 0 <= t - 2 < len(chunks):
            last[t - 2] = step_two(t - 2, again[t - 2])
        if 0 <= t - 3 < len(chunks):
            step_three(t - 3, last[t - 3])
    if len(outs) == 1:
        outs[0][...] = total_s[...]
    else:
        qkv_out, wo_out, up_out, down_out, tail_out = outs
        per, width = wo_out.shape
        spots = [(qkv_out, i) for i in range(3)] + [(wo_out, 0)] + [(up_out, i) for i in range(up_out.shape[1] // width)]
        for i, (ref, j) in enumerate(spots):
            ref[:, j * width:(j + 1) * width] = total_s[i * per:(i + 1) * per]
        top = len(spots) * per
        down_out[...] = total_s[top:top + down_out.shape[0]]
        tail_out[...] = total_s[top + down_out.shape[0]:]
    for copy in waiting + cores:
        copy.wait_send()
    row_copy.wait()


def scatter(dims, partials, rows_pair, out_shapes):
    rows, width = partials.shape[-2:]
    size_z, side, _ = dims
    parts = len(row_chunks(rows))
    across = max(parts * ((size_z - 1) + 2 * (side - 1)), 1)
    more = max(side - 1, 1)
    vmem = pl.BlockSpec(memory_space=pltpu.VMEM)
    any_spec = pl.BlockSpec(memory_space=pl.ANY)
    return pl.pallas_call(
        functools.partial(scatter_kernel, dims),
        out_shape=tuple(jax.ShapeDtypeStruct(shape, f32) for shape in out_shapes)
        + (jax.ShapeDtypeStruct(rows_pair.shape[1:], bf16),),
        in_specs=[vmem, any_spec],
        out_specs=(vmem,) * len(out_shapes) + (any_spec,),
        scratch_shapes=[
            pltpu.VMEM(dims + (rows, width), bf16),
            pltpu.VMEM(dims + (rows, width), bf16),
            pltpu.VMEM((more, size_z, side, rows, width), bf16),
            pltpu.VMEM((side, size_z, rows, width), bf16),
            pltpu.VMEM((more, size_z, rows, width), bf16),
            pltpu.VMEM((size_z, rows, width), bf16),
            pltpu.VMEM((max(size_z - 1, 1), rows, width), bf16),
            pltpu.VMEM((rows, width), f32),
            pltpu.SemaphoreType.DMA((2,)),
            pltpu.SemaphoreType.DMA((across,)),
            pltpu.SemaphoreType.DMA((across,)),
            pltpu.SemaphoreType.DMA((parts,)),
            pltpu.SemaphoreType.DMA((parts,)),
        ],
        compiler_params=pltpu.CompilerParams(collective_id=1, has_side_effects=True, vmem_limit_bytes=VMEM_BYTES),
        name="grad_scatter",
    )(partials, rows_pair)


def mm(left, right):
    return jnp.dot(left, right, preferred_element_type=f32)


def mm_t(left, right):
    return lax.dot_general(left, right, (((1,), (1,)), ((), ())), preferred_element_type=f32)


def t_mm(left, right):
    return lax.dot_general(left, right, (((0,), (0,)), ((), ())), preferred_element_type=f32)


def norm_parts(values):
    average = jnp.mean(values, axis=-1, keepdims=True)
    centered = values - average
    inverse = lax.rsqrt(jnp.mean(centered * centered, axis=-1, keepdims=True) + EPS)
    return centered * inverse, inverse


def norm_back(unit, inverse, gain, grad):
    scaled = grad * (1.0 + gain)
    mean_one = jnp.mean(scaled, axis=-1, keepdims=True)
    mean_two = jnp.mean(scaled * unit, axis=-1, keepdims=True)
    return (
        inverse * (scaled - mean_one - unit * mean_two),
        jnp.sum(grad * unit, axis=0, keepdims=True),
        jnp.sum(grad, axis=0, keepdims=True),
    )


def layers_kernel(seq, per, ff_per, rows_ref, cot_ref, *refs):
    fast = per is not None
    if fast:
        blocks_ref, out_ref, parts_ref, w_s, tail_s, f_s = refs[:6]
    else:
        w_s, down_all, tail_s, out_ref, gw_ref, gdown_ref, gtail_ref = refs[:7]
    h_s, a_s, q_s, o_s, z_s, n_s, g_s, slope_s, pf_s, dn_s, dy_s, dqkv_s, gt_s = refs[-13:]
    rows, width = cot_ref.shape
    ff = g_s.shape[-1]
    kinds = w_s.shape[1]
    down_at = kinds * per if fast else 0

    def down_part(e, c):
        if fast:
            group = width // ff_per
            return blocks_ref[e, c * group:(c + 1) * group, down_at:down_at + ff_per].reshape(width, width)
        return down_all[e, c * width:(c + 1) * width]

    def keep_grad(e, kind, value):
        if fast:
            f_s[kind] = value
        else:
            gw_ref[e, kind] = value.astype(bf16)

    def keep_down(e, c, value):
        if fast:
            group = width // ff_per
            for i in range(group):
                parts_ref[e, c * group + i, down_at:down_at + ff_per] = value[i * ff_per:(i + 1) * ff_per].astype(bf16)
        else:
            gdown_ref[e, c * width:(c + 1) * width] = value.astype(bf16)

    if fast:
        count = blocks_ref.shape[1]
        for e in range(2):
            tail_s[e] = jnp.zeros(tail_s.shape[1:], f32)

            @pl.loop(0, count // 2)
            def _(m, e=e):
                left = blocks_ref[e, 2 * m, 0:down_at].astype(f32)
                right = blocks_ref[e, 2 * m + 1, 0:down_at].astype(f32)
                at = pl.ds(pl.multiple_of(2 * per * m, 2 * per), 2 * per)
                for kind in range(kinds):
                    piece = slice(kind * per, (kind + 1) * per)
                    w_s[e, kind, at] = jnp.concatenate([left[piece], right[piece]], axis=0).astype(bf16)
                tail_s[e] += (
                    blocks_ref[e, 2 * m, down_at + ff_per:].astype(f32)
                    + blocks_ref[e, 2 * m + 1, down_at + ff_per:].astype(f32)
                )
    pairs = width // PAIR
    lane = lax.broadcasted_iota(jnp.int32, (rows, PAIR), 1)
    low_half = lane < HEAD_DIM
    key_ok = lax.broadcasted_iota(jnp.int32, (rows, rows), 1) < seq
    zero = jnp.zeros((rows, PAIR), bf16)

    def halves(values):
        return jnp.where(low_half, values, zero), jnp.where(low_half, zero, values)

    h_s[0] = rows_ref[...].astype(f32)

    @pl.loop(0, 2)
    def _(e):
        vec = tail_s[e, 0:8]
        bias = tail_s[e, 8:16]
        h = h_s[e]
        unit, _ = norm_parts(h)
        a = (unit * (1.0 + vec[0:1]) + vec[1:2]).astype(bf16)
        a_s[e] = a
        for third in range(3):
            cols = slice(third * width, (third + 1) * width)
            part = mm(a, w_s[e, third])
            if third != 1:
                part = part + vec[2 + third // 2:3 + third // 2]
            q_s[e, :, cols] = part.astype(bf16)
        for j in range(pairs):
            q = q_s[e, :, j * PAIR:(j + 1) * PAIR]
            k = q_s[e, :, width + j * PAIR:width + (j + 1) * PAIR]
            v = q_s[e, :, 2 * width + j * PAIR:2 * width + (j + 1) * PAIR]
            outs = []
            for i, q_half in enumerate(halves(q)):
                scores = jnp.where(key_ok, mm_t(q_half, k) * SCALE, -1e30)
                shifted = jnp.exp(scores - jnp.max(scores, axis=-1, keepdims=True))
                pf = shifted / jnp.sum(shifted, axis=-1, keepdims=True)
                pf_s[e, 2 * j + i] = pf
                outs.append(mm(pf.astype(bf16), v))
            o_s[e, :, j * PAIR:(j + 1) * PAIR] = jnp.where(low_half, outs[0], outs[1]).astype(bf16)
        z = h + mm(o_s[e], w_s[e, 3]) + vec[4:5]
        z_s[e] = z
        unit, _ = norm_parts(z)
        n = (unit * (1.0 + vec[5:6]) + vec[6:7]).astype(bf16)
        n_s[e] = n
        for c in range(ff // width):
            cols = slice(c * width, (c + 1) * width)
            u = mm(n, w_s[e, 4 + c]) + bias[c:c + 1]
            phi = 0.5 + 0.5 * lax.erf(u * (0.5 ** 0.5))
            g_s[e, :, cols] = (u * phi).astype(bf16)
            slope_s[e, :, cols] = phi + u * (jnp.exp(-0.5 * u * u) * 0.3989422804014327)
        total = z + vec[7:8]
        for c in range(ff // width):
            total = total + mm(g_s[e, :, c * width:(c + 1) * width], down_part(e, c))
        result = total.astype(bf16)
        out_ref[0] = result
        h_s[1] = jnp.where(e == 0, result.astype(f32), h_s[1])

    dy_s[...] = cot_ref[...].astype(f32)

    @pl.loop(0, 2)
    def _(step):
        e = 1 - step
        vec = tail_s[e, 0:8]
        dy = dy_s[...]
        dm = dy.astype(bf16)
        g7 = jnp.sum(dm.astype(f32), axis=0, keepdims=True)
        n = n_s[e]
        for c in range(ff // width):
            cols = slice(c * width, (c + 1) * width)
            keep_down(e, c, t_mm(g_s[e, :, cols], dm))
            du = (mm_t(dm, down_part(e, c)) * slope_s[e, :, cols]).astype(bf16)
            gt_s[8 + c:9 + c] = jnp.sum(du.astype(f32), axis=0, keepdims=True)
            keep_grad(e, 4 + c, t_mm(n, du))
            back = mm_t(du, w_s[e, 4 + c])
            if c == 0:
                dn_s[...] = back
            else:
                dn_s[...] += back
        unit, inverse = norm_parts(z_s[e])
        dz, g5, g6 = norm_back(unit, inverse, vec[5:6], dn_s[...])
        dz = dz + dy
        dr = dz.astype(bf16)
        g4 = jnp.sum(dr.astype(f32), axis=0, keepdims=True)
        keep_grad(e, 3, t_mm(o_s[e], dr))
        do_all = mm_t(dr, w_s[e, 3]).astype(bf16)
        for j in range(pairs):
            q = q_s[e, :, j * PAIR:(j + 1) * PAIR]
            k = q_s[e, :, width + j * PAIR:width + (j + 1) * PAIR]
            v = q_s[e, :, 2 * width + j * PAIR:2 * width + (j + 1) * PAIR]
            do = do_all[:, j * PAIR:(j + 1) * PAIR]
            dq, dk, dv = [], [], []
            for i, do_half in enumerate(halves(do)):
                pf = pf_s[e, 2 * j + i]
                dp = mm_t(do_half, v)
                ds = (pf * (dp - jnp.sum(pf * dp, axis=-1, keepdims=True))).astype(bf16)
                dv.append(t_mm(pf.astype(bf16), do))
                dq.append(mm(ds, k))
                dk.append(t_mm(ds, q))
            dqkv_s[:, j * PAIR:(j + 1) * PAIR] = (jnp.where(low_half, dq[0], dq[1]) * SCALE).astype(bf16)
            dqkv_s[:, width + j * PAIR:width + (j + 1) * PAIR] = (jnp.where(low_half, dk[0], dk[1]) * SCALE).astype(bf16)
            dqkv_s[:, 2 * width + j * PAIR:2 * width + (j + 1) * PAIR] = jnp.where(low_half, dv[0], dv[1]).astype(bf16)
        a = a_s[e]
        sums = []
        for third in range(3):
            cols = slice(third * width, (third + 1) * width)
            dpart = dqkv_s[:, cols]
            sums.append(jnp.sum(dpart.astype(f32), axis=0, keepdims=True))
            keep_grad(e, third, t_mm(a, dpart))
            back = mm_t(dpart, w_s[e, third])
            if third == 0:
                dn_s[...] = back
            else:
                dn_s[...] += back
        unit, inverse = norm_parts(h_s[e])
        dh, g0, g1 = norm_back(unit, inverse, vec[0:1], dn_s[...])
        low = (dz + dh).astype(bf16)
        out_ref[1] = low
        dy_s[...] = low.astype(f32)
        for row, value in enumerate((g0, g1, sums[0], sums[2], g4, g5, g6, g7)):
            gt_s[row:row + 1] = value
        if not fast:
            gtail_ref[e] = gt_s[...]
        else:
            @pl.loop(0, parts_ref.shape[1])
            def _(k):
                at = pl.ds(pl.multiple_of(per * k, per), per)
                for kind in range(0, kinds, 2):
                    both = jnp.concatenate([f_s[kind, at], f_s[kind + 1, at]], axis=0)
                    parts_ref[e, k, kind * per:(kind + 2) * per] = both.astype(bf16)
                parts_ref[e, k, down_at + ff_per:] = gt_s[...].astype(bf16)


def run_layers(seq, per, ff_per, rows, cot, weights, kinds, ff):
    t, width = rows.shape
    fast = per is not None
    vmem = pl.BlockSpec(memory_space=pltpu.VMEM)
    shape = jax.ShapeDtypeStruct
    outs = [shape((2, t, width), bf16)]
    outs += [shape(item.shape, bf16) for item in weights[:2]]
    if not fast:
        outs.append(shape(weights[2].shape, f32))
    extra = [
        pltpu.VMEM((2, kinds, width, width), bf16),
        pltpu.VMEM((2, 16, width), f32),
        pltpu.VMEM((kinds, width, width), f32),
    ]
    return pl.pallas_call(
        functools.partial(layers_kernel, seq, per, ff_per),
        out_shape=tuple(outs),
        in_specs=[vmem] * (2 + len(weights)),
        out_specs=(vmem,) * len(outs),
        scratch_shapes=(extra if fast else []) + [
            pltpu.VMEM((2, t, width), f32),
            pltpu.VMEM((2, t, width), bf16),
            pltpu.VMEM((2, t, 3 * width), bf16),
            pltpu.VMEM((2, t, width), bf16),
            pltpu.VMEM((2, t, width), f32),
            pltpu.VMEM((2, t, width), bf16),
            pltpu.VMEM((2, t, ff), bf16),
            pltpu.VMEM((2, t, ff), f32),
            pltpu.VMEM((2, HEADS, t, t), f32),
            pltpu.VMEM((t, width), f32),
            pltpu.VMEM((t, width), f32),
            pltpu.VMEM((t, 3 * width), bf16),
            pltpu.VMEM((16, width), f32),
        ],
        compiler_params=pltpu.CompilerParams(vmem_limit_bytes=VMEM_BYTES),
        name="two_layers",
    )(rows, cot, *weights)


def pack(count, pieces, down, tail):
    lead, kinds, width = pieces.shape[:-3], pieces.shape[-3], pieces.shape[-1]
    pieces = jnp.moveaxis(pieces.reshape(lead + (kinds, count, -1, width)), -4, -3)
    down = down.reshape(lead + (count, -1, width))
    tail = tail if tail.ndim == down.ndim else jnp.broadcast_to(tail[..., None, :, :], down.shape[:-2] + tail.shape[-2:])
    blocks = jnp.concatenate([pieces.reshape(lead + (count, -1, width)), down, tail.astype(bf16)], axis=-2)
    return jnp.pad(blocks, [(0, 0)] * (blocks.ndim - 2) + [(0, -blocks.shape[-2] % 16), (0, 0)])


def unpack(blocks, kinds, per, ff_per):
    lead, (count, _, width) = blocks.shape[:-3], blocks.shape[-3:]
    top = kinds * per
    pieces = blocks[..., :top, :].reshape(lead + (count, kinds, per, width))
    pieces = jnp.moveaxis(pieces, -3, -4).reshape(lead + (kinds, count * per, width))
    down = blocks[..., top:top + ff_per, :].reshape(lead + (count * ff_per, width))
    return pieces, down, blocks[..., top + ff_per:top + ff_per + 16, :]


def shards(dims, ends_in, vectors, up_bias, w_qkv, w_out, w_up, w_down):
    section_id = lax.axis_index("section")
    me = lax.axis_index("dp")
    is_first = section_id == 0
    local = ends_in[0]
    _, seq, width = local.shape
    count = dims[0] * dims[1] * dims[2]
    vec_rows, per = vectors.shape[1:]
    ff_per = up_bias.shape[1]
    ff = ff_per * count
    ups = ff // width
    kinds = 4 + ups
    fast = per % 8 == 0 and ff_per % 16 == 0 and width % ff_per == 0 and kinds % 2 == 0 and count % 2 == 0
    used = kinds * per + ff_per + 16
    rows = -(-used // 16) * 16
    t = -(-seq // 16) * 16
    padded = jnp.pad(local, ((0, 0), (0, t - seq), (0, 0)))

    def columns(matrix):
        return jnp.moveaxis(matrix.reshape(matrix.shape[0], -1, width), 1, 0)

    if fast:
        sources = (vectors[0], up_bias, w_qkv[0], w_out[0], w_up[0], w_down[0])
    else:
        tail = build_tail(me, vectors[0], up_bias, ups, width)
        pieces = jnp.concatenate([columns(w_qkv[0]), w_out[0][None], columns(w_up[0])])
        sources = (pack(1, pieces, w_down[0], tail)[0],)
    blocks, other = gather(dims, fast, sources, padded, rows, width)
    blocks = blocks.reshape(2, count, rows, width)
    own = lax.dynamic_index_in_dim(padded, section_id, 0, keepdims=False)
    x_rows = jnp.where(is_first, own, other)
    cot = jnp.where(is_first, other, own)
    if fast:
        pair, partials = run_layers(seq, per, ff_per, x_rows, cot, (blocks,), kinds, ff)
    else:
        pieces, down, tails = unpack(blocks, kinds, per, ff_per)
        tail = jnp.sum(tails.astype(f32), axis=1)
        pair, gpieces, gdown, gtail = run_layers(seq, None, None, x_rows, cot, (pieces, down, tail), kinds, ff)
        partials = pack(count, gpieces, gdown, gtail)
    partials = partials.reshape((2,) + dims + (rows, width))
    if fast:
        shapes = ((per, 3 * width), (per, width), (per, ff), (ff_per, width), (16, width))
        fqkv, fwo, fup, fdown, ftail, got = scatter(dims, partials, pair, shapes)
    else:
        total, got = scatter(dims, partials, pair, ((rows, width),))
        pieces, fdown, ftail = unpack(total[None], kinds, per, ff_per)
        ftail = ftail[0]
        fqkv = jnp.moveaxis(pieces[:3], 0, 1).reshape(per, 3 * width)
        fwo = pieces[3]
        fup = jnp.moveaxis(pieces[4:], 0, 1).reshape(per, ff)
    fvec = lax.dynamic_slice_in_dim(ftail[:vec_rows], me * per, per, 1)
    fbias = lax.dynamic_slice_in_dim(ftail[8:8 + ups].reshape(-1), me * ff_per, ff_per, 0)
    ends = jnp.stack([jnp.where(is_first, pair[1], got), jnp.where(is_first, got, pair[0])])[None, :, :seq]
    return ends, fvec[None], fbias[None], fqkv[None], fwo[None], fup[None], fdown[None]


def solution(mesh):
    dims = chip_grid(mesh.shape["dp"])
    specs = (
        P("section", "dp", None, None),
        P("section", None, "dp"),
        P("section", "dp"),
        P("section", "dp", None),
        P("section", "dp", None),
        P("section", "dp", None),
        P("section", "dp", None),
    )
    return jax.shard_map(
        functools.partial(shards, dims), mesh=mesh, in_specs=specs, out_specs=specs, check_vma=False
    )
```

```python
import functools

import jax
import jax.numpy as jnp
from jax import lax
from jax.experimental import pallas as pl
from jax.experimental.pallas import tpu as pltpu
from jax.sharding import PartitionSpec as P

HEADS = 6
HEAD_DIM = 64
PAIR = 2 * HEAD_DIM
EPS = 1e-06
SCALE = HEAD_DIM ** (-0.5)
GATHER_WEIGHTS = (1, 1)
GATHER_DEPTH = 2
SCATTER_WEIGHTS = (1, 1)
VMEM_BYTES = 56 * 1024 * 1024

bf16 = jnp.bfloat16
f32 = jnp.float32
MESH = pl.DeviceIdType.MESH


def chip_grid(count):
    for side in range(1, count + 1):
        if 2 * side**3 == count:
            return (2 * side, side, side)
    return (count, 1, 1)


def place(dims):
    me = lax.axis_index("dp")
    _, size_y, size_x = dims
    return me // (size_y * size_x), (me // size_x) % size_y, me % size_x


def rank(dims, z, y, x):
    return (z * dims[1] + y) * dims[2] + x


def greet(dims, s, z, y, x):
    barrier = pltpu.get_barrier_semaphore()
    count = 1
    pl.semaphore_signal(barrier, inc=1, device_id={"section": 1 - s}, device_id_type=MESH)
    for axis, (size, at) in enumerate(zip(dims, (z, y, x))):
        for d in range(1, size):
            there = [z, y, x]
            there[axis] = (at + d) % size
            pl.semaphore_signal(barrier, inc=1, device_id={"dp": rank(dims, *there)}, device_id_type=MESH)
            count += 1
    pl.semaphore_wait(barrier, count)


def row_groups(rows, weights):
    tiles, total = rows // 16, sum(weights)
    cuts = [tiles * sum(weights[:i]) // total for i in range(len(weights) + 1)]
    groups = []
    for low, high in zip(cuts, cuts[1:]):
        middle = (low + high + len(groups) % 2) // 2
        group = [(kind, pl.ds(16 * f, 16 * (l - f))) for kind, f, l in ((0, low, middle), (1, middle, high)) if l > f]
        if group:
            groups.append(group)
    return groups


def part_count(groups):
    return sum(len(group) for group in groups)


def selector(tall, wide, offset):
    row = lax.broadcasted_iota(jnp.int32, (tall, wide), 0)
    col = lax.broadcasted_iota(jnp.int32, (tall, wide), 1)
    return jnp.where(col == row + offset, 1.0, 0.0).astype(f32)


def build_shard(dims, vec_ref, bias_ref, qkv_ref, wo_ref, up_ref, down_ref, shard):
    per, width = wo_ref.shape
    ff_per = down_ref.shape[0]
    me = lax.axis_index("dp")
    ups = up_ref.shape[1] // width
    pieces = [qkv_ref[:, i * width:(i + 1) * width] for i in range(3)] + [wo_ref[...]]
    pieces += [up_ref[:, i * width:(i + 1) * width] for i in range(ups)]
    for i in range(0, len(pieces), 2):
        both = jnp.concatenate([pieces[i].astype(f32), pieces[i + 1].astype(f32)], axis=0)
        shard[i * per:(i + 2) * per] = both.astype(bf16)
    top = len(pieces) * per
    shard[top:top + ff_per] = down_ref[...]
    shard[top + ff_per:] = build_tail(me, vec_ref[...], bias_ref[...], ups, width).astype(bf16)


def build_tail(me, vec, bias, ups, width):
    per, ff_per = vec.shape[1], bias.shape[1]
    put = jnp.dot(vec.astype(f32), selector(per, width, me * per), preferred_element_type=f32)
    line = jnp.dot(jnp.broadcast_to(bias.astype(f32), (8, ff_per)), selector(ff_per, width, (me * ff_per) % width),
                   preferred_element_type=f32)
    at = lax.broadcasted_iota(jnp.int32, (8, width), 0)
    return jnp.concatenate([put, jnp.where(at == (me * ff_per) // width, line, 0.0)], axis=0)


def gather_kernel(dims, fast, *refs):
    if fast:
        vec_ref, bias_ref, qkv_ref, wo_ref, up_ref, down_ref, img_ref, out_ref, img_out, shard_ref = refs[:10]
    else:
        shard_ref, img_ref, out_ref, img_out = refs[:4]
    own_sem, img_sems, send_sems, recv_sems, core_send, core_recv = refs[-6:]
    size_z, side, _ = dims
    s = lax.axis_index("section")
    z, y, x = place(dims)
    if fast:
        build_shard(dims, vec_ref, bias_ref, qkv_ref, wo_ref, up_ref, down_ref, shard_ref)
    rows = shard_ref.shape[0]
    greet(dims, s, z, y, x)
    waiting = []
    arriving = []
    counter = [0, 0]

    def remote(src, dst, there):
        slot = counter[0]
        counter[0] += 1
        copy = pltpu.make_async_remote_copy(
            src_ref=src, dst_ref=dst, send_sem=send_sems.at[slot], recv_sem=recv_sems.at[slot],
            device_id={"dp": rank(dims, *there)}, device_id_type=MESH,
        )
        copy.start()
        waiting.append(copy)
        return copy

    def to_core(*at):
        slot = counter[1]
        counter[1] += 1
        for section, do_start in ((s, True), (1 - s, False)):
            piece = out_ref.at[(section,) + at]
            copy = pltpu.make_async_remote_copy(
                src_ref=piece, dst_ref=piece, send_sem=core_send.at[slot], recv_sem=core_recv.at[slot],
                device_id={"section": 1 - s}, device_id_type=MESH,
            )
            if do_start:
                copy.start()
                waiting.append(copy)
            else:
                arriving.append(copy)

    image = pltpu.make_async_remote_copy(
        src_ref=img_ref.at[1 - s], dst_ref=img_out, send_sem=img_sems.at[0], recv_sem=img_sems.at[1],
        device_id={"section": 1 - s}, device_id_type=MESH,
    )
    every = slice(None)
    groups = row_groups(rows, GATHER_WEIGHTS)

    def send_z(group):
        return [
            (kind, part, (z - d + size_z) % size_z,
             remote(shard_ref.at[part], out_ref.at[s, z, y, x, part], ((z + d) % size_z, y, x)))
            for kind, part in group for d in range(1, size_z)
        ]

    first, second, third = {}, {}, {}
    for c in range(min(GATHER_DEPTH, len(groups))):
        first[c] = send_z(groups[c])
    own = pltpu.make_async_copy(shard_ref, out_ref.at[s, z, y, x], own_sem)
    own.start()
    image.start()
    own.wait()
    to_core(z, y, x)
    for t in range(len(groups) + 2):
        if t < len(groups):
            for kind, part, at, copy in first[t]:
                copy.wait_recv()
            if t + GATHER_DEPTH < len(groups):
                first[t + GATHER_DEPTH] = send_z(groups[t + GATHER_DEPTH])
            second[t] = []
            for kind, part in groups[t]:
                piece = out_ref.at[s, every, y, x, part]
                for d in range(1, side):
                    there = (z, (y + d) % side, x) if kind == 0 else (z, y, (x + d) % side)
                    at = ((y if kind == 0 else x) - d + side) % side
                    second[t].append((kind, part, at, remote(piece, piece, there)))
            for kind, part, at, copy in first[t]:
                to_core(at, y, x, part)
        c = t - 1
        if 0 <= c < len(groups):
            for kind, part, at, copy in second[c]:
                copy.wait_recv()
            third[c] = []
            for kind, part in groups[c]:
                piece = out_ref.at[s, every, every, x, part] if kind == 0 else out_ref.at[s, every, y, every, part]
                for d in range(1, side):
                    there = (z, y, (x + d) % side) if kind == 0 else (z, (y + d) % side, x)
                    at = ((x if kind == 0 else y) - d + side) % side
                    third[c].append((kind, part, at, remote(piece, piece, there)))
            for kind, part, at, copy in second[c]:
                to_core(*((every, at, x, part) if kind == 0 else (every, y, at, part)))
        c = t - 2
        if 0 <= c < len(groups):
            for kind, part, at, copy in third[c]:
                copy.wait_recv()
                to_core(*((every, every, at, part) if kind == 0 else (every, at, every, part)))
    for copy in waiting:
        copy.wait_send()
    for copy in arriving:
        copy.wait_recv()
    image.wait()


def gather(dims, fast, sources, images, rows, width):
    size_z, side, _ = dims
    parts = part_count(row_groups(rows, GATHER_WEIGHTS))
    across = parts * ((size_z - 1) + 2 * (side - 1))
    any_spec = pl.BlockSpec(memory_space=pl.ANY)
    vmem = pl.BlockSpec(memory_space=pltpu.VMEM)
    sems = [
        pltpu.SemaphoreType.DMA,
        pltpu.SemaphoreType.DMA((2,)),
        pltpu.SemaphoreType.DMA((max(across, 1),)),
        pltpu.SemaphoreType.DMA((max(across, 1),)),
        pltpu.SemaphoreType.DMA((across + 1,)),
        pltpu.SemaphoreType.DMA((across + 1,)),
    ]
    return pl.pallas_call(
        functools.partial(gather_kernel, dims, fast),
        out_shape=(
            jax.ShapeDtypeStruct((2,) + dims + (rows, width), bf16),
            jax.ShapeDtypeStruct(images.shape[1:], bf16),
        ),
        in_specs=[vmem] * len(sources) + [any_spec] if fast else [any_spec] * 2,
        out_specs=(any_spec, any_spec),
        scratch_shapes=([pltpu.VMEM((rows, width), bf16)] if fast else []) + sems,
        compiler_params=pltpu.CompilerParams(collective_id=0, has_side_effects=True, vmem_limit_bytes=VMEM_BYTES),
        name="weight_gather",
    )(*sources, images)


def scatter_kernel(dims, part_ref, rows_ref, *refs):
    outs, rows_out = refs[:-14], refs[-14]
    (core_in, work, in_one, two, in_two, three, in_three, total_s,
     row_sems, send_sems, recv_sems, core_send, core_recv) = refs[-13:]
    size_z, side, _ = dims
    s = lax.axis_index("section")
    z, y, x = place(dims)
    rows = total_s.shape[0]
    every = slice(None)
    greet(dims, s, z, y, x)
    waiting = []
    counter = [0]

    def remote(src, dst, there):
        slot = counter[0]
        counter[0] += 1
        copy = pltpu.make_async_remote_copy(
            src_ref=src, dst_ref=dst, send_sem=send_sems.at[slot], recv_sem=recv_sems.at[slot],
            device_id={"dp": rank(dims, *there)}, device_id_type=MESH,
        )
        copy.start()
        waiting.append(copy)
        return copy

    groups = row_groups(rows, SCATTER_WEIGHTS)
    cores = []
    for group in groups:
        for kind, part in group:
            slot = len(cores)
            copy = pltpu.make_async_remote_copy(
                src_ref=part_ref.at[1 - s, :, :, :, part], dst_ref=core_in.at[:, :, :, part],
                send_sem=core_send.at[slot], recv_sem=core_recv.at[slot],
                device_id={"section": 1 - s}, device_id_type=MESH,
            )
            copy.start()
            cores.append(copy)
    row_copy = pltpu.make_async_remote_copy(
        src_ref=rows_ref.at[s], dst_ref=rows_out, send_sem=row_sems.at[0], recv_sem=row_sems.at[1],
        device_id={"section": 1 - s}, device_id_type=MESH,
    )
    row_copy.start()
    core_at = [0]

    def step_core(group):
        for kind, part in group:
            cores[core_at[0]].wait_recv()
            core_at[0] += 1

            @pl.loop(0, size_z * side)
            def _(i, part=part):
                u, v = i // side, i % side
                for w in range(side):
                    work[u, v, w, part] = (
                        part_ref[s, u, v, w, part].astype(f32) + core_in[u, v, w, part].astype(f32)
                    ).astype(bf16)

    def send_one(group):
        sent = []
        for kind, part in group:
            for d in range(1, side):
                at = ((x if kind == 0 else y) + d) % side
                src, there = (work.at[:, :, at, part], (z, y, at)) if kind == 0 else (work.at[:, at, :, part], (z, at, x))
                sent.append(remote(src, in_one.at[d - 1, :, :, part], there))
        return sent

    def step_one(group):
        for kind, part in group:
            @pl.loop(0, size_z)
            def _(u, kind=kind, part=part):
                for v in range(side):
                    at = (u, v, x) if kind == 0 else (u, y, v)
                    total = work[at + (part,)].astype(f32)
                    for d in range(1, side):
                        total = total + in_one[d - 1, u, v, part].astype(f32)
                    two[v, u, part] = total.astype(bf16)

        sent = []
        for kind, part in group:
            for d in range(1, side):
                at = ((y if kind == 0 else x) + d) % side
                there = (z, at, x) if kind == 0 else (z, y, at)
                sent.append(remote(two.at[at, :, part], in_two.at[d - 1, :, part], there))
        return sent

    def step_two(group):
        for kind, part in group:
            for u in range(size_z):
                total = two[y if kind == 0 else x, u, part].astype(f32)
                for d in range(1, side):
                    total = total + in_two[d - 1, u, part].astype(f32)
                three[u, part] = total.astype(bf16)

        return [
            remote(three.at[(z + d) % size_z, part], in_three.at[d - 1, part], ((z + d) % size_z, y, x))
            for kind, part in group for d in range(1, size_z)
        ]

    def step_three(group):
        for kind, part in group:
            total = three[z, part].astype(f32)
            for d in range(1, size_z):
                total = total + in_three[d - 1, part].astype(f32)
            total_s[part] = total

    step_core(groups[0])
    one, again, last = {0: send_one(groups[0])}, {}, {}
    for t in range(len(groups) + 2):
        if t + 1 < len(groups):
            step_core(groups[t + 1])
        if t < len(groups):
            for copy in one[t]:
                copy.wait_recv()
            if t + 1 < len(groups):
                one[t + 1] = send_one(groups[t + 1])
            again[t] = step_one(groups[t])
        if 0 <= t - 1 < len(groups):
            for copy in again[t - 1]:
                copy.wait_recv()
            last[t - 1] = step_two(groups[t - 1])
        if 0 <= t - 2 < len(groups):
            for copy in last[t - 2]:
                copy.wait_recv()
            step_three(groups[t - 2])
    if len(outs) == 1:
        outs[0][...] = total_s[...]
    else:
        qkv_out, wo_out, up_out, down_out, tail_out = outs
        per, width = wo_out.shape
        spots = [(qkv_out, i) for i in range(3)] + [(wo_out, 0)] + [(up_out, i) for i in range(up_out.shape[1] // width)]
        for i, (ref, j) in enumerate(spots):
            ref[:, j * width:(j + 1) * width] = total_s[i * per:(i + 1) * per]
        top = len(spots) * per
        down_out[...] = total_s[top:top + down_out.shape[0]]
        tail_out[...] = total_s[top + down_out.shape[0]:]
    for copy in waiting + cores:
        copy.wait_send()
    row_copy.wait()


def scatter(dims, partials, rows_pair, out_shapes):
    rows, width = partials.shape[-2:]
    size_z, side, _ = dims
    parts = part_count(row_groups(rows, SCATTER_WEIGHTS))
    across = max(parts * ((size_z - 1) + 2 * (side - 1)), 1)
    more = max(side - 1, 1)
    vmem = pl.BlockSpec(memory_space=pltpu.VMEM)
    any_spec = pl.BlockSpec(memory_space=pl.ANY)
    return pl.pallas_call(
        functools.partial(scatter_kernel, dims),
        out_shape=tuple(jax.ShapeDtypeStruct(shape, f32) for shape in out_shapes)
        + (jax.ShapeDtypeStruct(rows_pair.shape[1:], bf16),),
        in_specs=[vmem, any_spec],
        out_specs=(vmem,) * len(out_shapes) + (any_spec,),
        scratch_shapes=[
            pltpu.VMEM(dims + (rows, width), bf16),
            pltpu.VMEM(dims + (rows, width), bf16),
            pltpu.VMEM((more, size_z, side, rows, width), bf16),
            pltpu.VMEM((side, size_z, rows, width), bf16),
            pltpu.VMEM((more, size_z, rows, width), bf16),
            pltpu.VMEM((size_z, rows, width), bf16),
            pltpu.VMEM((max(size_z - 1, 1), rows, width), bf16),
            pltpu.VMEM((rows, width), f32),
            pltpu.SemaphoreType.DMA((2,)),
            pltpu.SemaphoreType.DMA((across,)),
            pltpu.SemaphoreType.DMA((across,)),
            pltpu.SemaphoreType.DMA((parts,)),
            pltpu.SemaphoreType.DMA((parts,)),
        ],
        compiler_params=pltpu.CompilerParams(collective_id=1, has_side_effects=True, vmem_limit_bytes=VMEM_BYTES),
        name="grad_scatter",
    )(partials, rows_pair)


def mm(left, right):
    return jnp.dot(left, right, preferred_element_type=f32)


def mm_t(left, right):
    return lax.dot_general(left, right, (((1,), (1,)), ((), ())), preferred_element_type=f32)


def t_mm(left, right):
    return lax.dot_general(left, right, (((0,), (0,)), ((), ())), preferred_element_type=f32)


def norm_parts(values):
    average = jnp.mean(values, axis=-1, keepdims=True)
    centered = values - average
    inverse = lax.rsqrt(jnp.mean(centered * centered, axis=-1, keepdims=True) + EPS)
    return centered * inverse, inverse


def norm_back(unit, inverse, gain, grad):
    scaled = grad * (1.0 + gain)
    mean_one = jnp.mean(scaled, axis=-1, keepdims=True)
    mean_two = jnp.mean(scaled * unit, axis=-1, keepdims=True)
    return (
        inverse * (scaled - mean_one - unit * mean_two),
        jnp.sum(grad * unit, axis=0, keepdims=True),
        jnp.sum(grad, axis=0, keepdims=True),
    )


def layer_steps(dims, seq, per, ff_per, rows_ref, cot_ref, refs):
    fast = per is not None
    if fast:
        blocks_ref, out_ref, parts_ref, w_s, tail_s, f_s = refs[:6]
    else:
        w_s, down_all, tail_s, out_ref, gw_ref, gdown_ref, gtail_ref = refs[:7]
    h_s, a_s, q_s, o_s, z_s, n_s, g_s, slope_s, pf_s, dn_s, dy_s, dqkv_s, gt_s = refs[-13:]
    rows, width = cot_ref.shape
    ff = g_s.shape[-1]
    kinds = w_s.shape[1]
    down_at = kinds * per if fast else 0

    def at_rank(e, k):
        _, size_y, size_x = dims
        return e, k // (size_y * size_x), (k // size_x) % size_y, k % size_x

    def down_part(e, c):
        if fast:
            group = width // ff_per
            rows_of = pl.ds(down_at, ff_per)
            return jnp.concatenate([blocks_ref[at_rank(e, c * group + i) + (rows_of,)] for i in range(group)], axis=0)
        return down_all[e, c * width:(c + 1) * width]

    def keep_grad(e, kind, value):
        if fast:
            f_s[kind] = value
        else:
            gw_ref[e, kind] = value.astype(bf16)

    def keep_down(e, c, value):
        if fast:
            group = width // ff_per
            for i in range(group):
                parts_ref[at_rank(e, c * group + i) + (pl.ds(down_at, ff_per),)] = value[i * ff_per:(i + 1) * ff_per].astype(bf16)
        else:
            gdown_ref[e, c * width:(c + 1) * width] = value.astype(bf16)

    def prepare(e):
        count = dims[0] * dims[1] * dims[2]
        tail_s[e] = jnp.zeros(tail_s.shape[1:], f32)

        @pl.loop(0, count // 2)
        def _(m):
            first, second = at_rank(e, 2 * m), at_rank(e, 2 * m + 1)
            top, rest = pl.ds(0, down_at), pl.ds(down_at + ff_per, 16)
            left = blocks_ref[first + (top,)].astype(f32)
            right = blocks_ref[second + (top,)].astype(f32)
            at = pl.ds(pl.multiple_of(2 * per * m, 2 * per), 2 * per)
            for kind in range(kinds):
                piece = slice(kind * per, (kind + 1) * per)
                w_s[e, kind, at] = jnp.concatenate([left[piece], right[piece]], axis=0).astype(bf16)
            tail_s[e] += blocks_ref[first + (rest,)].astype(f32) + blocks_ref[second + (rest,)].astype(f32)

    pairs = width // PAIR
    lane = lax.broadcasted_iota(jnp.int32, (rows, PAIR), 1)
    low_half = lane < HEAD_DIM
    key_ok = lax.broadcasted_iota(jnp.int32, (rows, rows), 1) < seq
    zero = jnp.zeros((rows, PAIR), bf16)

    def halves(values):
        return jnp.where(low_half, values, zero), jnp.where(low_half, zero, values)

    def forward(e):
        if e == 0:
            h_s[0] = rows_ref[...].astype(f32)
        vec = tail_s[e, 0:8]
        bias = tail_s[e, 8:16]
        h = h_s[e]
        unit, _ = norm_parts(h)
        a = (unit * (1.0 + vec[0:1]) + vec[1:2]).astype(bf16)
        a_s[e] = a
        for third in range(3):
            cols = slice(third * width, (third + 1) * width)
            part = mm(a, w_s[e, third])
            if third != 1:
                part = part + vec[2 + third // 2:3 + third // 2]
            q_s[e, :, cols] = part.astype(bf16)
        for j in range(pairs):
            q = q_s[e, :, j * PAIR:(j + 1) * PAIR]
            k = q_s[e, :, width + j * PAIR:width + (j + 1) * PAIR]
            v = q_s[e, :, 2 * width + j * PAIR:2 * width + (j + 1) * PAIR]
            outs = []
            for i, q_half in enumerate(halves(q)):
                scores = jnp.where(key_ok, mm_t(q_half, k) * SCALE, -1e30)
                shifted = jnp.exp(scores - jnp.max(scores, axis=-1, keepdims=True))
                pf = shifted / jnp.sum(shifted, axis=-1, keepdims=True)
                pf_s[e, 2 * j + i] = pf
                outs.append(mm(pf.astype(bf16), v))
            o_s[e, :, j * PAIR:(j + 1) * PAIR] = jnp.where(low_half, outs[0], outs[1]).astype(bf16)
        z = h + mm(o_s[e], w_s[e, 3]) + vec[4:5]
        z_s[e] = z
        unit, _ = norm_parts(z)
        n = (unit * (1.0 + vec[5:6]) + vec[6:7]).astype(bf16)
        n_s[e] = n
        for c in range(ff // width):
            cols = slice(c * width, (c + 1) * width)
            u = mm(n, w_s[e, 4 + c]) + bias[c:c + 1]
            phi = 0.5 + 0.5 * lax.erf(u * (0.5 ** 0.5))
            g_s[e, :, cols] = (u * phi).astype(bf16)
            slope_s[e, :, cols] = phi + u * (jnp.exp(-0.5 * u * u) * 0.3989422804014327)
        total = z + vec[7:8]
        for c in range(ff // width):
            total = total + mm(g_s[e, :, c * width:(c + 1) * width], down_part(e, c))
        result = total.astype(bf16)
        out_ref[0] = result
        if e == 0:
            h_s[1] = result.astype(f32)

    def backward(e):
        if e == 1:
            dy_s[...] = cot_ref[...].astype(f32)
        vec = tail_s[e, 0:8]
        dy = dy_s[...]
        dm = dy.astype(bf16)
        g7 = jnp.sum(dm.astype(f32), axis=0, keepdims=True)
        n = n_s[e]
        for c in range(ff // width):
            cols = slice(c * width, (c + 1) * width)
            keep_down(e, c, t_mm(g_s[e, :, cols], dm))
            du = (mm_t(dm, down_part(e, c)) * slope_s[e, :, cols]).astype(bf16)
            gt_s[8 + c:9 + c] = jnp.sum(du.astype(f32), axis=0, keepdims=True)
            keep_grad(e, 4 + c, t_mm(n, du))
            back = mm_t(du, w_s[e, 4 + c])
            if c == 0:
                dn_s[...] = back
            else:
                dn_s[...] += back
        unit, inverse = norm_parts(z_s[e])
        dz, g5, g6 = norm_back(unit, inverse, vec[5:6], dn_s[...])
        dz = dz + dy
        dr = dz.astype(bf16)
        g4 = jnp.sum(dr.astype(f32), axis=0, keepdims=True)
        keep_grad(e, 3, t_mm(o_s[e], dr))
        do_all = mm_t(dr, w_s[e, 3]).astype(bf16)
        for j in range(pairs):
            q = q_s[e, :, j * PAIR:(j + 1) * PAIR]
            k = q_s[e, :, width + j * PAIR:width + (j + 1) * PAIR]
            v = q_s[e, :, 2 * width + j * PAIR:2 * width + (j + 1) * PAIR]
            do = do_all[:, j * PAIR:(j + 1) * PAIR]
            dq, dk, dv = [], [], []
            for i, do_half in enumerate(halves(do)):
                pf = pf_s[e, 2 * j + i]
                dp = mm_t(do_half, v)
                ds = (pf * (dp - jnp.sum(pf * dp, axis=-1, keepdims=True))).astype(bf16)
                dv.append(t_mm(pf.astype(bf16), do))
                dq.append(mm(ds, k))
                dk.append(t_mm(ds, q))
            dqkv_s[:, j * PAIR:(j + 1) * PAIR] = (jnp.where(low_half, dq[0], dq[1]) * SCALE).astype(bf16)
            dqkv_s[:, width + j * PAIR:width + (j + 1) * PAIR] = (jnp.where(low_half, dk[0], dk[1]) * SCALE).astype(bf16)
            dqkv_s[:, 2 * width + j * PAIR:2 * width + (j + 1) * PAIR] = jnp.where(low_half, dv[0], dv[1]).astype(bf16)
        a = a_s[e]
        sums = []
        for third in range(3):
            cols = slice(third * width, (third + 1) * width)
            dpart = dqkv_s[:, cols]
            sums.append(jnp.sum(dpart.astype(f32), axis=0, keepdims=True))
            keep_grad(e, third, t_mm(a, dpart))
            back = mm_t(dpart, w_s[e, third])
            if third == 0:
                dn_s[...] = back
            else:
                dn_s[...] += back
        unit, inverse = norm_parts(h_s[e])
        dh, g0, g1 = norm_back(unit, inverse, vec[0:1], dn_s[...])
        low = (dz + dh).astype(bf16)
        out_ref[1] = low
        dy_s[...] = low.astype(f32)
        for row, value in enumerate((g0, g1, sums[0], sums[2], g4, g5, g6, g7)):
            gt_s[row:row + 1] = value
        if not fast:
            gtail_ref[e] = gt_s[...]
        else:
            @pl.loop(0, dims[0] * dims[1] * dims[2])
            def _(k):
                at = pl.ds(pl.multiple_of(per * k, per), per)
                block = at_rank(e, k)
                for kind in range(0, kinds, 2):
                    both = jnp.concatenate([f_s[kind, at], f_s[kind + 1, at]], axis=0)
                    parts_ref[block + (pl.ds(kind * per, 2 * per),)] = both.astype(bf16)
                parts_ref[block + (pl.ds(down_at + ff_per, 16),)] = gt_s[...].astype(bf16)

    return prepare, forward, backward


def layers_kernel(seq, rows_ref, cot_ref, *refs):
    _, forward, backward = layer_steps(None, seq, None, None, rows_ref, cot_ref, refs)
    forward(0)
    forward(1)
    backward(1)
    backward(0)


def layer_scratch(t, width, ff):
    return [
        pltpu.VMEM((2, t, width), f32),
        pltpu.VMEM((2, t, width), bf16),
        pltpu.VMEM((2, t, 3 * width), bf16),
        pltpu.VMEM((2, t, width), bf16),
        pltpu.VMEM((2, t, width), f32),
        pltpu.VMEM((2, t, width), bf16),
        pltpu.VMEM((2, t, ff), bf16),
        pltpu.VMEM((2, t, ff), f32),
        pltpu.VMEM((2, HEADS, t, t), f32),
        pltpu.VMEM((t, width), f32),
        pltpu.VMEM((t, width), f32),
        pltpu.VMEM((t, 3 * width), bf16),
        pltpu.VMEM((16, width), f32),
    ]


def run_layers(seq, rows, cot, weights, ff):
    t, width = rows.shape
    vmem = pl.BlockSpec(memory_space=pltpu.VMEM)
    shape = jax.ShapeDtypeStruct
    outs = [shape((2, t, width), bf16)]
    outs += [shape(item.shape, bf16) for item in weights[:2]]
    outs.append(shape(weights[2].shape, f32))
    return pl.pallas_call(
        functools.partial(layers_kernel, seq),
        out_shape=tuple(outs),
        in_specs=[vmem] * (2 + len(weights)),
        out_specs=(vmem,) * len(outs),
        scratch_shapes=layer_scratch(t, width, ff),
        compiler_params=pltpu.CompilerParams(vmem_limit_bytes=VMEM_BYTES),
        name="two_layers",
    )(rows, cot, *weights)


def whole_kernel(dims, seq, per, ff_per, *refs):
    (vec_ref, bias_ref, qkv_ref, wo_ref, up_ref, down_ref, img_ref,
     qkv_out, wo_out, up_out, down_out, tail_out, ends_out) = refs[:13]
    (shard_ref, io, blocks, parts, pair, core_in, work, in_one, two, in_two, three, in_three, total_s) = refs[13:26]
    img_sems, end_sems, g_send, g_recv, gc_send, gc_recv, send_sems, recv_sems, core_send, core_recv = refs[26:36]
    layer_refs = refs[36:]
    size_z, side, _ = dims
    s = lax.axis_index("section")
    z, y, x = place(dims)
    build_shard(dims, vec_ref, bias_ref, qkv_ref, wo_ref, up_ref, down_ref, shard_ref)
    rows, width = shard_ref.shape
    prepare, forward, backward = layer_steps(
        dims, seq, per, ff_per, io.at[0], io.at[1], (blocks, pair, parts) + layer_refs
    )
    every = slice(None)
    io[s] = img_ref[s]
    blocks[s, z, y, x] = shard_ref[...]
    waiting = []
    counter = [0, 0, 0]

    def chips(which, sends, recvs, src, dst, there):
        slot = counter[which]
        counter[which] += 1
        copy = pltpu.make_async_remote_copy(
            src_ref=src, dst_ref=dst, send_sem=sends.at[slot], recv_sem=recvs.at[slot],
            device_id={"dp": rank(dims, *there)}, device_id_type=MESH,
        )
        waiting.append(copy)
        return copy

    def cores(src, dst, send, recv):
        return pltpu.make_async_remote_copy(
            src_ref=src, dst_ref=dst, send_sem=send, recv_sem=recv, device_id={"section": 1 - s}, device_id_type=MESH,
        )

    def to_core(*at):
        slot = counter[1]
        counter[1] += 1
        mine, other = blocks.at[(s,) + at], blocks.at[(1 - s,) + at]
        sent = cores(mine, mine, gc_send.at[slot], gc_recv.at[slot])
        waiting.append(sent)
        return sent, cores(other, other, gc_send.at[slot], gc_recv.at[slot])

    groups = row_groups(rows, GATHER_WEIGHTS)
    flat = [item for group in groups for item in group]
    first, second, third = [], [], []
    for kind, part in flat:
        first.append([
            (chips(0, g_send, g_recv, shard_ref.at[part], blocks.at[s, z, y, x, part], ((z + d) % size_z, y, x)),
             to_core((z - d + size_z) % size_z, y, x, part))
            for d in range(1, size_z)
        ])
    for kind, part in flat:
        piece = blocks.at[s, every, y, x, part]
        hops = []
        for d in range(1, side):
            there = (z, (y + d) % side, x) if kind == 0 else (z, y, (x + d) % side)
            at = ((y if kind == 0 else x) - d + side) % side
            hops.append((chips(0, g_send, g_recv, piece, piece, there),
                         to_core(*((every, at, x, part) if kind == 0 else (every, y, at, part)))))
        second.append(hops)
    for kind, part in flat:
        piece = blocks.at[s, every, every, x, part] if kind == 0 else blocks.at[s, every, y, every, part]
        hops = []
        for d in range(1, side):
            there = (z, y, (x + d) % side) if kind == 0 else (z, (y + d) % side, x)
            at = ((x if kind == 0 else y) - d + side) % side
            hops.append((chips(0, g_send, g_recv, piece, piece, there),
                         to_core(*((every, every, at, part) if kind == 0 else (every, at, every, part)))))
        third.append(hops)
    own = to_core(z, y, x)
    image = cores(img_ref.at[1 - s], io.at[s], img_sems.at[0], img_sems.at[1])
    image_in = cores(img_ref.at[1 - s], io.at[1 - s], img_sems.at[0], img_sems.at[1])

    def begin(hops):
        for copy, _ in hops:
            copy.start()

    def pass_on(hops):
        for copy, (sent, _) in hops:
            copy.wait_recv()
            sent.start()

    def arrive(hops):
        for _, (_, got) in hops:
            got.wait_recv()

    def scatter_copies():
        cut = [item for group in row_groups(rows, SCATTER_WEIGHTS) for item in group]
        out = []
        for slot, (kind, part) in enumerate(cut):
            core = cores(parts.at[1 - s, :, :, :, part], core_in.at[:, :, :, part], core_send.at[slot], core_recv.at[slot])
            one, again, last = [], [], []
            for d in range(1, side):
                at = ((x if kind == 0 else y) + d) % side
                src, there = (work.at[:, :, at, part], (z, y, at)) if kind == 0 else (work.at[:, at, :, part], (z, at, x))
                one.append(chips(2, send_sems, recv_sems, src, in_one.at[d - 1, :, :, part], there))
            for d in range(1, side):
                at = ((y if kind == 0 else x) + d) % side
                there = (z, at, x) if kind == 0 else (z, y, at)
                again.append(chips(2, send_sems, recv_sems, two.at[at, :, part], in_two.at[d - 1, :, part], there))
            for d in range(1, size_z):
                at = (z + d) % size_z
                last.append(chips(2, send_sems, recv_sems, three.at[at, part], in_three.at[d - 1, part], (at, y, x)))
            waiting.append(core)
            out.append((kind, part, core, one, again, last))
        return out

    cut = scatter_copies()

    def start_cores():
        for _, _, core, _, _, _ in cut:
            core.start()

    def add_cores():
        for kind, part, core, one, _, _ in cut:
            core.wait_recv()

            @pl.loop(0, size_z * side)
            def _(i, part=part):
                u, v = i // side, i % side
                for w in range(side):
                    work[u, v, w, part] = (
                        parts[s, u, v, w, part].astype(f32) + core_in[u, v, w, part].astype(f32)
                    ).astype(bf16)

            for copy in one:
                copy.start()

    def step_one(item):
        kind, part, _, one, again, _ = item
        for copy in one:
            copy.wait_recv()

        @pl.loop(0, size_z)
        def _(u):
            for v in range(side):
                at = (u, v, x) if kind == 0 else (u, y, v)
                total = work[at + (part,)].astype(f32)
                for d in range(1, side):
                    total = total + in_one[d - 1, u, v, part].astype(f32)
                two[v, u, part] = total.astype(bf16)

        for copy in again:
            copy.start()

    def step_two(item):
        kind, part, _, _, again, last = item
        for copy in again:
            copy.wait_recv()
        for u in range(size_z):
            total = two[y if kind == 0 else x, u, part].astype(f32)
            for d in range(1, side):
                total = total + in_two[d - 1, u, part].astype(f32)
            three[u, part] = total.astype(bf16)
        for copy in last:
            copy.start()

    def step_three(item):
        _, part, _, _, _, last = item
        for copy in last:
            copy.wait_recv()
        total = three[z, part].astype(f32)
        for d in range(1, size_z):
            total = total + in_three[d - 1, part].astype(f32)
        total_s[part] = total

    greet(dims, s, z, y, x)

    @pl.when(s == 1)
    def _():
        for hops in first:
            arrive(hops)

    for hops in first:
        begin(hops)
    image.start()
    own[0].start()
    for near, far in zip(first, second):
        pass_on(near)
        begin(far)
    for near, far in zip(second, third):
        pass_on(near)
        begin(far)

    def finish():
        for hops in third:
            pass_on(hops)

    @pl.when(s == 0)
    def _():
        finish()

    @pl.when(s == 1)
    def _():
        own[1].wait_recv()
        for hops in second + third:
            arrive(hops)

    image_in.wait_recv()
    prepare(0)
    forward(0)

    @pl.when(s == 1)
    def _():
        finish()

    @pl.when(s == 0)
    def _():
        own[1].wait_recv()
        for hops in first + second + third:
            arrive(hops)

    prepare(1)
    forward(1)
    backward(1)

    @pl.when(s == 0)
    def _():
        start_cores()

    @pl.when(s == 1)
    def _():
        add_cores()

    backward(0)
    end = cores(pair.at[s], ends_out.at[s], end_sems.at[0], end_sems.at[1])
    end_in = cores(pair.at[s], ends_out.at[1 - s], end_sems.at[0], end_sems.at[1])

    @pl.when(s == 1)
    def _():
        start_cores()

    @pl.when(s == 0)
    def _():
        add_cores()

    end.start()
    ends_out[s] = pair[1 - s]
    for step in (step_one, step_two, step_three):
        for item in cut:
            step(item)
    spots = [(qkv_out, i) for i in range(3)] + [(wo_out, 0)] + [(up_out, i) for i in range(up_out.shape[1] // width)]
    for i, (ref, j) in enumerate(spots):
        ref[:, j * width:(j + 1) * width] = total_s[i * per:(i + 1) * per]
    top = len(spots) * per
    down_out[...] = total_s[top:top + ff_per]
    tail_out[...] = total_s[top + ff_per:]
    for copy in waiting:
        copy.wait_send()
    image.wait_send()
    end.wait_send()
    end_in.wait_recv()


def run_whole(dims, seq, sources, images, rows, kinds, ff):
    per, width = sources[3].shape
    ff_per = sources[5].shape[0]
    t = images.shape[1]
    size_z, side, _ = dims
    hops = (size_z - 1) + 2 * (side - 1)
    g_parts = part_count(row_groups(rows, GATHER_WEIGHTS))
    s_parts = part_count(row_groups(rows, SCATTER_WEIGHTS))
    more = max(side - 1, 1)
    vmem = pl.BlockSpec(memory_space=pltpu.VMEM)
    dma = pltpu.SemaphoreType.DMA
    shape = jax.ShapeDtypeStruct
    return pl.pallas_call(
        functools.partial(whole_kernel, dims, seq, per, ff_per),
        out_shape=(
            shape((per, 3 * width), f32), shape((per, width), f32), shape((per, ff), f32), shape((ff_per, width), f32),
            shape((16, width), f32), shape(images.shape, bf16),
        ),
        in_specs=[vmem] * 7,
        out_specs=(vmem,) * 6,
        scratch_shapes=[
            pltpu.VMEM((rows, width), bf16),
            pltpu.VMEM((2, t, width), bf16),
            pltpu.VMEM((2,) + dims + (rows, width), bf16),
            pltpu.VMEM((2,) + dims + (rows, width), bf16),
            pltpu.VMEM((2, t, width), bf16),
            pltpu.VMEM(dims + (rows, width), bf16),
            pltpu.VMEM(dims + (rows, width), bf16),
            pltpu.VMEM((more, size_z, side, rows, width), bf16),
            pltpu.VMEM((side, size_z, rows, width), bf16),
            pltpu.VMEM((more, size_z, rows, width), bf16),
            pltpu.VMEM((size_z, rows, width), bf16),
            pltpu.VMEM((max(size_z - 1, 1), rows, width), bf16),
            pltpu.VMEM((rows, width), f32),
            dma((2,)), dma((2,)),
            dma((max(g_parts * hops, 1),)), dma((max(g_parts * hops, 1),)),
            dma((g_parts * hops + 1,)), dma((g_parts * hops + 1,)),
            dma((max(s_parts * hops, 1),)), dma((max(s_parts * hops, 1),)),
            dma((s_parts,)), dma((s_parts,)),
            pltpu.VMEM((2, kinds, width, width), bf16),
            pltpu.VMEM((2, 16, width), f32),
            pltpu.VMEM((kinds, width, width), f32),
        ] + layer_scratch(t, width, ff),
        compiler_params=pltpu.CompilerParams(collective_id=2, has_side_effects=True, vmem_limit_bytes=VMEM_BYTES),
        name="whole_step",
    )(*sources, images)


def pack(count, pieces, down, tail):
    lead, kinds, width = pieces.shape[:-3], pieces.shape[-3], pieces.shape[-1]
    pieces = jnp.moveaxis(pieces.reshape(lead + (kinds, count, -1, width)), -4, -3)
    down = down.reshape(lead + (count, -1, width))
    tail = tail if tail.ndim == down.ndim else jnp.broadcast_to(tail[..., None, :, :], down.shape[:-2] + tail.shape[-2:])
    blocks = jnp.concatenate([pieces.reshape(lead + (count, -1, width)), down, tail.astype(bf16)], axis=-2)
    return jnp.pad(blocks, [(0, 0)] * (blocks.ndim - 2) + [(0, -blocks.shape[-2] % 16), (0, 0)])


def unpack(blocks, kinds, per, ff_per):
    lead, (count, _, width) = blocks.shape[:-3], blocks.shape[-3:]
    top = kinds * per
    pieces = blocks[..., :top, :].reshape(lead + (count, kinds, per, width))
    pieces = jnp.moveaxis(pieces, -3, -4).reshape(lead + (kinds, count * per, width))
    down = blocks[..., top:top + ff_per, :].reshape(lead + (count * ff_per, width))
    return pieces, down, blocks[..., top + ff_per:top + ff_per + 16, :]


def shards(dims, ends_in, vectors, up_bias, w_qkv, w_out, w_up, w_down):
    section_id = lax.axis_index("section")
    me = lax.axis_index("dp")
    is_first = section_id == 0
    local = ends_in[0]
    _, seq, width = local.shape
    count = dims[0] * dims[1] * dims[2]
    vec_rows, per = vectors.shape[1:]
    ff_per = up_bias.shape[1]
    ff = ff_per * count
    ups = ff // width
    kinds = 4 + ups
    fast = per % 8 == 0 and ff_per % 16 == 0 and width % ff_per == 0 and kinds % 2 == 0 and count % 2 == 0
    used = kinds * per + ff_per + 16
    rows = -(-used // 16) * 16
    t = -(-seq // 16) * 16
    padded = jnp.pad(local, ((0, 0), (0, t - seq), (0, 0)))

    def columns(matrix):
        return jnp.moveaxis(matrix.reshape(matrix.shape[0], -1, width), 1, 0)

    if fast:
        sources = (vectors[0], up_bias, w_qkv[0], w_out[0], w_up[0], w_down[0])
        fqkv, fwo, fup, fdown, ftail, ends = run_whole(dims, seq, sources, padded, rows, kinds, ff)
    else:
        tail = build_tail(me, vectors[0], up_bias, ups, width)
        pieces = jnp.concatenate([columns(w_qkv[0]), w_out[0][None], columns(w_up[0])])
        sources = (pack(1, pieces, w_down[0], tail)[0],)
        blocks, other = gather(dims, False, sources, padded, rows, width)
        own = lax.dynamic_index_in_dim(padded, section_id, 0, keepdims=False)
        x_rows = jnp.where(is_first, own, other)
        cot = jnp.where(is_first, other, own)
        pieces, down, tails = unpack(blocks.reshape(2, count, rows, width), kinds, per, ff_per)
        tail = jnp.sum(tails.astype(f32), axis=1)
        pair, gpieces, gdown, gtail = run_layers(seq, x_rows, cot, (pieces, down, tail), ff)
        partials = pack(count, gpieces, gdown, gtail).reshape((2,) + dims + (rows, width))
        total, got = scatter(dims, partials, pair, ((rows, width),))
        pieces, fdown, ftail = unpack(total[None], kinds, per, ff_per)
        ftail = ftail[0]
        fqkv = jnp.moveaxis(pieces[:3], 0, 1).reshape(per, 3 * width)
        fwo = pieces[3]
        fup = jnp.moveaxis(pieces[4:], 0, 1).reshape(per, ff)
        ends = jnp.stack([jnp.where(is_first, pair[1], got), jnp.where(is_first, got, pair[0])])
    fvec = lax.dynamic_slice_in_dim(ftail[:vec_rows], me * per, per, 1)
    fbias = lax.dynamic_slice_in_dim(ftail[8:8 + ups].reshape(-1), me * ff_per, ff_per, 0)
    return ends[None, :, :seq], fvec[None], fbias[None], fqkv[None], fwo[None], fup[None], fdown[None]


def solution(mesh):
    dims = chip_grid(mesh.shape["dp"])
    specs = (
        P("section", "dp", None, None),
        P("section", None, "dp"),
        P("section", "dp"),
        P("section", "dp", None),
        P("section", "dp", None),
        P("section", "dp", None),
        P("section", "dp", None),
    )
    return jax.shard_map(
        functools.partial(shards, dims), mesh=mesh, in_specs=specs, out_specs=specs, check_vma=False
    )
```
